128 devices in a mesh: gx: 8 (over x_lo, y), gy: 4 (over x_hi, core), sa: 4 (over z).
Axes of the slice: x: 4 (x_hi: 2, x_lo: 2; x = x_hi * 2 + x_lo), y: 4, z: 4, core: 2. Of those that a mesh axis runs over, the one named last changes fastest.
Arguments:
- field: float32 [48, 2, 2048, 1024], P('sa', None, 'gx', 'gy'), may hold values from -6.8 to 6.8
- basis_species: float32 [48, 24], replicated, may hold values from -5 to 5
- basis_x: float32 [2048, 256], P('gx'), may hold values from -5 to 5
- basis_y: float32 [1024, 256], P(('gy', 'sa')), may hold values from -5 to 5
Outputs:
- core: float32 [256, 256, 24, 2], P(('gy', 'sa'), 'gx')
- factor_species: float32 [48, 24], replicated
- factor_x: float32 [2048, 256], P('gx')
- factor_y: float32 [1024, 256], P(('gy', 'sa'))
The draws below stay inside these ranges and needn't reach their ends.
All inputs are finite; a program needn't handle non-finite values.
Results may differ from the reference program's by a relative error of at most 0.0003.
Values sent between devices are 32-bit elements; how exact they have to be, the bound alone decides.
No kernel may reach another device: no remote copies, remote signals or barrier semaphores. Data moves between devices by JAX's collectives and lax.ppermute only.
A program may use at most 128 MiB of HBM per device.

```python
import jax
import jax.numpy as jnp
from jax import lax

NS = 48
P_SIZE = 2
RS = 24
R1 = 256
R2 = 256
NX = 2048
NY = 1024


def draw_field(key, part):
    key = jax.random.fold_in(key, 11)
    keys = jax.random.split(key, 1)
    values = jnp.clip(jax.random.normal(keys[0], (NS, P_SIZE, NX, NY), jnp.float32), -4.0, 4.0)
    return values


def shard_levels(rng, dims, cuts, least, largest):
    level, own = 1.0, jax.random.fold_in(rng, 6)
    for position, parts in cuts:
        heights = jnp.exp(jax.random.uniform(jax.random.fold_in(own, position), (parts,), jnp.float32, least / len(cuts), largest / len(cuts)))
        level = level * jnp.repeat(heights, dims[position] // parts).reshape([-1 if axis == position else 1 for axis in range(len(dims))])
    return level


def centred(rng, dims, spread, most, pieces=(), dtype=jnp.bfloat16):
    gain = shard_levels(rng, dims, pieces, -0.22, 0.18) if pieces else 1.0
    drawn = jax.random.normal(rng, dims, jnp.float32) * spread * gain
    return jnp.minimum(jnp.maximum(drawn, -most), most).astype(dtype)


def setup_inputs(seed: int = 0) -> dict:
    key_of = jax.random.split(jax.random.key(seed), 5)
    field = draw_field(jax.random.fold_in(key_of[4], 71), 0)
    basis_species = centred(key_of[1], (NS, RS), 1.0, 5.0, (), jnp.float32)
    basis_x = centred(key_of[2], (NX, R1), 1.0, 5.0, ((0, 8),), jnp.float32)
    basis_y = centred(key_of[3], (NY, R2), 1.0, 5.0, ((0, 16),), jnp.float32)
    return {"field": field, "basis_species": basis_species, "basis_x": basis_x, "basis_y": basis_y}


def orthonormal(image):
    norms = jnp.dot(image.T, image, precision=lax.Precision.HIGHEST)
    lower = jnp.linalg.cholesky(norms)
    return jax.scipy.linalg.solve_triangular(lower, image.T, lower=True).T

def reference(field, basis_species, basis_x, basis_y):
    high = lax.Precision.HIGHEST
    flat = field.reshape(field.shape[0], -1)
    gram_species = jnp.dot(flat, flat.T, precision=high)
    factor_species = orthonormal(jnp.dot(gram_species, basis_species, precision=high))
    first = jnp.einsum('spxy,sr->rpxy', field, factor_species, precision=high)
    gram_x = jnp.einsum('rpxy,rpzy->xz', first, first, precision=high)
    factor_x = orthonormal(jnp.dot(gram_x, basis_x, precision=high))
    second = jnp.einsum('rpxy,xq->rpqy', first, factor_x, precision=high)
    gram_y = jnp.einsum('rpqy,rpqz->yz', second, second, precision=high)
    factor_y = orthonormal(jnp.dot(gram_y, basis_y, precision=high))
    core = jnp.einsum('rpqy,yt->tqrp', second, factor_y, precision=high)
    return (core, factor_species, factor_x, factor_y)
```

```python
import functools

import jax
import jax.numpy as jnp
from jax import lax
from jax.experimental import pallas as pl
from jax.experimental.pallas import tpu as pltpu
from jax.sharding import Mesh
from jax.sharding import PartitionSpec as P

F32 = jnp.float32
BF16 = jnp.bfloat16
HIGH = lax.Precision.HIGHEST
GX = ("xl", "y")
GY = ("xh", "c")
VMEM = pl.BlockSpec(memory_space=pltpu.VMEM)
SMEM = pl.BlockSpec(memory_space=pltpu.SMEM)
PARAMS = pltpu.CompilerParams(vmem_limit_bytes=48 * 1024 * 1024)

NN = (((1,), (0,)), ((), ()))
NT = (((1,), (1,)), ((), ()))
TN = (((0,), (0,)), ((), ()))


def exact(a, b, dims=NN):
    return lax.dot_general(a, b, dims, precision=HIGH, preferred_element_type=F32)


def split(a):
    hi = a.astype(BF16)
    return hi, (a - hi.astype(F32)).astype(BF16)


def dot3(a, b, dims=NN):
    one = functools.partial(lax.dot_general, dimension_numbers=dims, preferred_element_type=F32)
    return one(a[0], b[0]) + (one(a[0], b[1]) + one(a[1], b[0]))


def iota(shape, dim):
    return lax.broadcasted_iota(jnp.int32, shape, dim)


def invert_block(block):
    n = block.shape[0]
    unit = (iota((n, n), 0) == iota((n, n), 1)).astype(F32)
    work = jnp.concatenate([block, unit], axis=1)
    rows = []
    for j in range(n):
        base = (j // 8) * 8
        local = j - base
        pivot = work[local : local + 1, :]
        scaled = pivot * (1.0 / pivot[:, j : j + 1])
        rows.append(pivot[:, n:] * lax.rsqrt(pivot[:, j : j + 1]))
        if j + 1 < n:
            if local == 7:
                work = work[8:, :]
            work = work - work[:, j : j + 1] * scaled
    return jnp.concatenate(rows, axis=0)


def invert_factor(work_ref, n, size):
    for k in range(0, n, size):
        inner = invert_block(work_ref[k : k + size, k : k + size])
        row = exact(inner, work_ref[k : k + size, :])
        work_ref[k : k + size, :] = row
        if k + size < n:
            work_ref[k + size :, :] -= exact(row[:, k + size : n], row, TN)
    return work_ref[:, n:]


def fill(work_ref, norms):
    n = norms.shape[0]
    work_ref[:, :n] = norms
    work_ref[:, n:] = (iota((n, n), 0) == iota((n, n), 1)).astype(F32)


def pack_kernel(field_ref, out_ref):
    planes = field_ref.shape[1]
    for p in range(planes):
        turned = field_ref[0, p].T
        out_ref[:, 0, p] = turned.reshape(out_ref.shape[0], 8, turned.shape[1])


def pack(field, groups):
    species, planes, rows, cols = field.shape
    return pl.pallas_call(
        pack_kernel,
        grid=(species,),
        in_specs=[pl.BlockSpec((1, planes, rows, cols), lambda s: (s, 0, 0, 0))],
        out_specs=pl.BlockSpec((groups, 1, planes, 8, rows), lambda s: (0, s, 0, 0, 0)),
        out_shape=jax.ShapeDtypeStruct((groups, species, planes, 8, rows), F32),
        compiler_params=PARAMS,
        name="pack",
    )(field)


def gram_kernel(cells_ref, out_ref, acc_ref):
    step = pl.program_id(0) * pl.num_programs(1) + pl.program_id(1)

    @pl.when(step == 0)
    def _():
        acc_ref[...] = jnp.zeros_like(acc_ref)

    count = acc_ref.shape[0]
    cells = cells_ref[...].reshape(count, cells_ref.shape[-1])
    hi, lo = split(cells)
    twice = (lo.astype(F32) * 2.0).astype(BF16)
    one = functools.partial(lax.dot_general, dimension_numbers=NT, preferred_element_type=F32)
    acc_ref[...] += one(hi, hi) + one(hi, twice)

    @pl.when(step == pl.num_programs(0) * pl.num_programs(1) - 1)
    def _():
        same = (iota((count, count), 0) % 8) == (iota((count, count), 1) % 8)
        kept = jnp.where(same, acc_ref[...], 0.0)
        pick = (iota((count, 128), 0) // 8 == iota((count, 128), 1)).astype(F32)
        summed = exact(exact(pick, kept, TN), pick)
        both = 0.5 * (summed + summed.T)
        out_ref[...] = both[: out_ref.shape[0], :]


def gram(cells):
    sa, gx, own, planes, eight, width = cells.shape
    species = sa * own
    return pl.pallas_call(
        gram_kernel,
        grid=(gx, planes),
        in_specs=[pl.BlockSpec((sa, 1, own, 1, eight, width), lambda g, p: (0, g, 0, p, 0, 0))],
        out_specs=pl.BlockSpec((species, 128), lambda g, p: (0, 0)),
        out_shape=jax.ShapeDtypeStruct((species, 128), F32),
        scratch_shapes=[pltpu.VMEM((species * 8, species * 8), F32)],
        compiler_params=PARAMS,
        name="gram_species",
    )(cells)


def first_kernel(grams_ref, basis_s_ref, basis_x_ref, cells_ref, factor_ref, first_ref, image_ref, hold_ref):
    sa, gx, own, planes, eight, width = cells_ref.shape
    species, rank = basis_s_ref.shape
    gram_all = jnp.sum(grams_ref[...], axis=0)[:, :species]
    image = exact(gram_all, basis_s_ref[...])
    norms = exact(image, image, TN)
    factor = exact(image, invert_block(norms), NT)
    factor_ref[...] = factor
    low, wide = rank * 8, species * 8
    rep_r = (iota((low, rank), 0) // 8 == iota((low, rank), 1)).astype(F32)
    rep_s = (iota((species, wide), 0) == iota((species, wide), 1) // 8).astype(F32)
    mixed = exact(exact(rep_r, factor, NT), rep_s)
    same = (iota((low, wide), 0) % 8) == (iota((low, wide), 1) % 8)
    mix = split(jnp.where(same, mixed, 0.0))
    hold_ref[...] = jnp.zeros_like(hold_ref)

    @pl.loop(0, gx)
    def _(g):
        basis = split(basis_x_ref[g])
        for p in range(planes):
            cells = split(cells_ref[:, g, :, p].reshape(wide, width))
            first = dot3(mix, cells)
            first_ref[g, p * low : (p + 1) * low, :] = first
            hold_ref[p * low : (p + 1) * low, :] += dot3(split(first), basis)

    turned = split(hold_ref[...].T)

    @pl.loop(0, gx)
    def _(g):
        image_ref[g] = dot3(turned, split(first_ref[g]))


def first_stage(grams, basis_s, basis_x, cells):
    sa, gx, own, planes, eight, width = cells.shape
    species, rank = basis_s.shape
    low = rank * 8
    return pl.pallas_call(
        first_kernel,
        in_specs=[VMEM] * 4,
        out_specs=[VMEM] * 3,
        out_shape=[
            jax.ShapeDtypeStruct((species, rank), F32),
            jax.ShapeDtypeStruct((gx, planes * low, width), F32),
            jax.ShapeDtypeStruct((gx, basis_x.shape[2], width), F32),
        ],
        scratch_shapes=[pltpu.VMEM((planes * low, basis_x.shape[2]), F32)],
        compiler_params=PARAMS,
        name="first_and_image_x",
    )(grams, basis_s, basis_x, cells)


def second_kernel(place_ref, image_ref, first_ref, factor_ref, send_ref, work_ref, hold_ref):
    gx, rank, width = image_ref.shape
    n = rank
    work_ref[...] = jnp.zeros_like(work_ref)
    hold_ref[...] = jnp.zeros_like(hold_ref)

    @pl.loop(0, gx)
    def _(g):
        image = image_ref[g]
        both = split(image)
        work_ref[:, :n] += exact(image, image, NT)
        hold_ref[...] += dot3(split(first_ref[g]), both, NT)

    work_ref[:, n:] = (iota((n, n), 0) == iota((n, n), 1)).astype(F32)
    inverse = invert_factor(work_ref, n, 64)
    factor_ref[...] = exact(inverse, image_ref[place_ref[0]]).T
    second = exact(hold_ref[...], inverse, NT)
    hold_ref[...] = second
    groups = send_ref.shape[0] // gx
    each = 3
    lane = iota((8, 128), 1)
    for g in range(groups):
        for half in range(n // 128):
            tiles = [
                hold_ref[(g * each + j) * 8 : (g * each + j + 1) * 8, half * 128 : (half + 1) * 128]
                for j in range(each)
            ]
            for part in range(4):
                moved = [
                    tile if (j - part) % 4 == 0 else pltpu.roll(tile, ((j - part) % 4) * 32, 1)
                    for j, tile in enumerate(tiles)
                ]
                mixed = jnp.where(lane < 32, moved[0], jnp.where(lane < 64, moved[1], moved[2]))
                send_ref[g * gx + half * 4 + part] = jnp.where(lane < 96, mixed, 0.0)


def second_stage(place, image, first):
    gx, rank, width = image.shape
    rows = first.shape[1]
    return pl.pallas_call(
        second_kernel,
        in_specs=[SMEM, VMEM, VMEM],
        out_specs=[VMEM] * 2,
        out_shape=[
            jax.ShapeDtypeStruct((width, rank), F32),
            jax.ShapeDtypeStruct((rows // 24 * gx, 8, 128), F32),
        ],
        scratch_shapes=[pltpu.VMEM((rank, 2 * rank), F32), pltpu.VMEM((rows, rank), F32)],
        compiler_params=PARAMS,
        name="factor_x_and_second",
    )(place, image, first)


def image_y_kernel(second_ref, basis_ref, image_ref):
    turned = second_ref[...].T
    both = split(turned)
    inner = dot3(both, split(basis_ref[...]))
    left = split(inner.T)
    blocks, rank, width = image_ref.shape
    for b in range(blocks):
        cols = slice(b * width, (b + 1) * width)
        image_ref[b] = dot3(left, (both[0][:, cols], both[1][:, cols]))


def image_y_stage(second, basis_y):
    rows, rank = basis_y.shape
    return pl.pallas_call(
        image_y_kernel,
        in_specs=[VMEM] * 2,
        out_specs=VMEM,
        out_shape=jax.ShapeDtypeStruct((rows // 256, rank, 256), F32),
        compiler_params=PARAMS,
        name="image_y",
    )(second, basis_y)


def core_kernel(place_ref, image_ref, second_ref, factor_ref, core_ref, work_ref, turn_ref):
    blocks, n, width = image_ref.shape
    norms = jnp.zeros((n, n), F32)
    raw = jnp.zeros((n, second_ref.shape[1]), F32)
    for b in range(blocks):
        image = image_ref[b]
        norms += exact(image, image, NT)
        raw += exact(image, second_ref[b * width : (b + 1) * width, :])
    fill(work_ref, norms)
    inverse = invert_factor(work_ref, n, 64)
    core_ref[...] = exact(inverse, raw)
    turn_ref[...] = exact(inverse, image_ref[place_ref[0]]).T
    count = factor_ref.shape[0]
    factor_ref[...] = turn_ref[pl.ds(pl.multiple_of(place_ref[1] * count, count), count), :]


def core_stage(place, image, second, count):
    blocks, n, width = image.shape
    return pl.pallas_call(
        core_kernel,
        in_specs=[SMEM, VMEM, VMEM],
        out_specs=[VMEM] * 2,
        out_shape=[
            jax.ShapeDtypeStruct((count, n), F32),
            jax.ShapeDtypeStruct((n, second.shape[1]), F32),
        ],
        scratch_shapes=[pltpu.VMEM((n, 2 * n), F32), pltpu.VMEM((width, n), F32)],
        compiler_params=PARAMS,
        name="factor_y_and_core",
    )(place, image, second)


def swap(parts, axes):
    return lax.all_to_all(parts, axes, split_axis=0, concat_axis=0, tiled=True)


def spread(one, axes, count):
    return swap(jnp.broadcast_to(one, (count,) + one.shape), axes)


def total(partial):
    chips = GX + ("xh", "z")
    size = partial.size // 256
    mine = jnp.sum(swap(partial.reshape(2, size // 2, 256), "c"), axis=0)
    mine = jnp.sum(swap(mine.reshape(64, size // 128, 256), chips), axis=0)
    half = spread(mine, chips, 64)
    return spread(half, "c", 2).reshape(partial.shape)


def local(field, basis_s, basis_x, basis_y):
    gx_n, sa_n = 8, 4
    basis_x_all = lax.all_gather(basis_x, GX, axis=0)
    basis_y_all = lax.all_gather(basis_y, GY + ("z",), axis=0, tiled=True)
    cells = swap(pack(field, gx_n * sa_n), ("z",) + GX)
    cells = cells.reshape((sa_n, gx_n) + cells.shape[1:])
    partial = jnp.sum(spread(gram(cells), GX, gx_n), axis=0)
    grams = spread(partial, GY + ("z",), 16)
    factor_s, first, image_part = first_stage(grams, basis_s, basis_x_all, cells)
    image_x = total(image_part)
    gx = lax.axis_index(GX)
    factor_x, send = second_stage(jnp.reshape(gx, (1,)), image_x, first)
    second = swap(send, GY + ("z",) + GX).reshape(-1, 128)
    image_y = total(image_y_stage(second, basis_y_all))
    place = jnp.stack([lax.axis_index(GY), lax.axis_index("z")])
    factor_y, core = core_stage(place, image_y, second, basis_y.shape[0])
    rank_y = core.shape[0]
    blocks = swap(core.reshape(16, rank_y // 16, 128), GY + ("z",))
    core = blocks.reshape(2, 8, rank_y // 16, 4, 32)[:, :, :, :3, :]
    core = core.transpose(2, 4, 1, 3, 0).reshape(rank_y // 16, 32, 24, 2)
    return core, factor_s, factor_x, factor_y


def solution(mesh):
    fine = Mesh(mesh.devices.reshape(2, 4, 2, 2, 4), ("xl", "y", "xh", "c", "z"))
    yz = GY + ("z",)
    return jax.shard_map(
        local,
        mesh=fine,
        in_specs=(P("z", None, GX, GY), P(), P(GX, None), P(yz, None)),
        out_specs=(P(yz, GX, None, None), P(), P(GX, None), P(yz, None)),
        check_vma=False,
    )
```

```python
import functools

import jax
import jax.numpy as jnp
from jax import lax
from jax.experimental import pallas as pl
from jax.experimental.pallas import tpu as pltpu
from jax.sharding import Mesh
from jax.sharding import PartitionSpec as P

F32 = jnp.float32
BF16 = jnp.bfloat16
HIGH = lax.Precision.HIGHEST
GX = ("xl", "y")
GY = ("xh", "c")
CHIPS = GX + ("xh", "z")
VMEM = pl.BlockSpec(memory_space=pltpu.VMEM)
SMEM = pl.BlockSpec(memory_space=pltpu.SMEM)
HBM = pl.BlockSpec(memory_space=pltpu.HBM)
PARAMS = pltpu.CompilerParams(vmem_limit_bytes=20 * 1024 * 1024)

NN = (((1,), (0,)), ((), ()))
NT = (((1,), (1,)), ((), ()))
TN = (((0,), (0,)), ((), ()))


def exact(a, b, dims=NN):
    return lax.dot_general(a, b, dims, precision=HIGH, preferred_element_type=F32)


def split(a):
    hi = a.astype(BF16)
    return hi, (a - hi.astype(F32)).astype(BF16)


def dot3(a, b, dims=NN):
    one = functools.partial(lax.dot_general, dimension_numbers=dims, preferred_element_type=F32)
    return one(a[0], b[0]) + (one(a[0], b[1]) + one(a[1], b[0]))


def iota(shape, dim):
    return lax.broadcasted_iota(jnp.int32, shape, dim)


def invert_block(block):
    n = block.shape[0]
    unit = (iota((n, n), 0) == iota((n, n), 1)).astype(F32)
    parts = [block, unit]
    if 2 * n < 128:
        parts.append(jnp.zeros((n, 128 - 2 * n), F32))
    work = jnp.concatenate(parts, axis=1)
    tiles = [work[i : i + 8, :] for i in range(0, n, 8)]
    full = (8, 128)
    sub = iota(full, 0)
    out = []
    for j, own in enumerate(tiles):
        rows = [jnp.broadcast_to(own[t : t + 1, :], full) for t in range(8)]
        columns = [
            [jnp.broadcast_to(tile[:, 8 * j + t : 8 * j + t + 1], full) for t in range(8)] for tile in tiles[j:]
        ]
        cells = {
            (t, u): jnp.broadcast_to(columns[0][u][t : t + 1, :], full) for t in range(8) for u in range(t, 8)
        }
        columns = columns[1:]
        done = jnp.zeros(full, F32)
        for t in range(8):
            inverse = 1.0 / cells[t, t]
            for u in range(t + 1, 8):
                share = cells[t, u] * inverse
                for v in range(u, 8):
                    cells[u, v] = cells[u, v] - share * cells[t, v]
                rows[u] = rows[u] - share * rows[t]
            for column in columns:
                share = column[t] * inverse
                for u in range(t + 1, 8):
                    column[u] = column[u] - share * cells[t, u]
                column[t] = share
            done = jnp.where(sub == t, rows[t] * lax.rsqrt(cells[t, t]), done)
        out.append(done)
        for i, column in enumerate(columns):
            tile = tiles[j + 1 + i]
            for t in range(8):
                tile = tile - column[t] * rows[t]
            tiles[j + 1 + i] = tile
    return jnp.concatenate(out, axis=0)[:, n : 2 * n]


def invert_factor(work_ref, n, size):
    for k in range(0, n, size):
        inner = invert_block(work_ref[k : k + size, k : k + size])
        row = exact(inner, work_ref[k : k + size, :])
        work_ref[k : k + size, :] = row
        if k + size < n:
            work_ref[k + size :, :] -= exact(row[:, k + size : n], row, TN)
    return work_ref[:, n:]


def fill(work_ref, norms):
    n = norms.shape[0]
    work_ref[:, :n] = norms
    work_ref[:, n:] = (iota((n, n), 0) == iota((n, n), 1)).astype(F32)


def pack_kernel(field_ref, out_ref, held_ref, turned_ref, in_sems, out_sems):
    species, planes, rows, cols = held_ref.shape
    coming = [pltpu.make_async_copy(field_ref.at[s], held_ref.at[s], in_sems.at[s]) for s in range(species)]
    going = [pltpu.make_async_copy(turned_ref.at[:, s], out_ref.at[:, s], out_sems.at[s]) for s in range(species)]
    for copy in coming:
        copy.start()
    for s in range(species):
        coming[s].wait()
        for p in range(planes):
            turned_ref[:, s, p] = held_ref[s, p].T.reshape(out_ref.shape[0], 8, rows)
        going[s].start()
    for copy in going:
        copy.wait()


def pack(field, groups):
    species, planes, rows, cols = field.shape
    shape = (groups, species, planes, 8, rows)
    return pl.pallas_call(
        pack_kernel,
        in_specs=[HBM],
        out_specs=HBM,
        out_shape=jax.ShapeDtypeStruct(shape, F32),
        scratch_shapes=[
            pltpu.VMEM(field.shape, F32),
            pltpu.VMEM(shape, F32),
            pltpu.SemaphoreType.DMA((species,)),
            pltpu.SemaphoreType.DMA((species,)),
        ],
        compiler_params=PARAMS,
        cost_estimate=cost(0, 8 * field.size),
        name="pack",
    )(pltpu.with_memory_space_constraint(field, pltpu.HBM))


def cost(flops, size):
    return pl.CostEstimate(flops=flops, bytes_accessed=size, transcendentals=0)


def bring(cells_ref, held_ref, sems):
    copies = [
        pltpu.make_async_copy(cells_ref.at[:, g], held_ref.at[:, g], sems.at[g]) for g in range(cells_ref.shape[1])
    ]
    for copy in copies:
        copy.start()
    return copies


def held(cells):
    return [pltpu.VMEM(cells.shape, F32), pltpu.SemaphoreType.DMA((cells.shape[1],))]


def planes_of(cells_ref, g):
    sa, gx, own, planes, eight, width = cells_ref.shape
    return [cells_ref[:, g, :, p].reshape(sa * own * eight, width) for p in range(planes)]


def gram_kernel(cells_ref, out_ref, acc_ref, held_ref, sems):
    copies = bring(cells_ref, held_ref, sems)
    count = acc_ref.shape[0]
    one = functools.partial(lax.dot_general, dimension_numbers=NT, preferred_element_type=F32)
    for g in range(cells_ref.shape[1]):
        copies[g].wait()
        hi, lo = split(jnp.concatenate(planes_of(held_ref, g), axis=1))
        twice = (lo.astype(F32) * 2.0).astype(BF16)
        part = one(hi, hi) + one(hi, twice)
        acc_ref[...] = part if g == 0 else acc_ref[...] + part
    same = (iota((count, count), 0) % 8) == (iota((count, count), 1) % 8)
    kept = jnp.where(same, acc_ref[...], 0.0)
    pick = (iota((count, 128), 0) // 8 == iota((count, 128), 1)).astype(F32)
    summed = exact(exact(pick, kept, TN), pick)
    both = 0.5 * (summed + summed.T)
    out_ref[...] = fold(both, count // 16)


def fold(both, half):
    row, lane = iota((half, 128), 0), iota((half, 128), 1)
    upper = both[:half, :]
    lower = pltpu.roll(both[half : 2 * half, :], 128 - half, 1)
    corner = jnp.where(row <= lane, upper, lower)
    full = jnp.where(lane < 2 * half, jnp.where(lane < half, corner, upper), 0.0)
    diagonal = jnp.sum(jnp.where(row == lane, lower, 0.0), axis=0, keepdims=True)
    rest = jnp.concatenate([full[16:half], jnp.broadcast_to(diagonal, (32 - half, 128))], axis=0)
    return full[:16] + pltpu.roll(rest, 64, 1)


def unfold(folded, half):
    rest = pltpu.roll(folded, 64, 1)
    full = jnp.concatenate([folded, rest[: half - 16]], axis=0)
    row, lane = iota((half, half), 0), iota((half, half), 1)
    corner, middle = full[:, :half], full[:, half : 2 * half]
    diagonal = jnp.broadcast_to(rest[half - 16 : half - 15, :half], (half, half))
    above = jnp.where(row <= lane, corner, 0.0)
    below = jnp.where(row > lane, corner, 0.0)
    first = above + jnp.where(row < lane, corner, 0.0).T
    last = below + below.T + jnp.where(row == lane, diagonal, 0.0)
    top = jnp.concatenate([first, middle], axis=1)
    return jnp.concatenate([top, jnp.concatenate([middle.T, last], axis=1)], axis=0)


def gram(cells):
    sa, gx, own, planes, eight, width = cells.shape
    species = sa * own
    return pl.pallas_call(
        gram_kernel,
        in_specs=[HBM],
        out_specs=VMEM,
        out_shape=jax.ShapeDtypeStruct((16, 128), F32),
        scratch_shapes=[pltpu.VMEM((species * 8, species * 8), F32)] + held(cells),
        compiler_params=PARAMS,
        cost_estimate=cost(4 * gx * planes * width * (8 * species) ** 2, 4 * cells.size),
        name="gram_species",
    )(pltpu.with_memory_space_constraint(cells, pltpu.HBM))


def based_kernel(place_ref, near_ref, far_ref, near_o_ref, far_o_ref, cells_ref, out_ref, held_ref, sems):
    xl, y, c = place_ref[0], place_ref[1], place_ref[2]
    quarter = near_ref.shape[0]
    copies = bring(cells_ref, held_ref, sems)
    for g in range(cells_ref.shape[1]):
        away = lax.rem(lax.rem(g, quarter) - y + quarter, quarter)
        here = g // quarter == xl
        own = jnp.where(here, near_ref[away], far_ref[away])
        other = jnp.where(here, near_o_ref[away], far_o_ref[away])
        both = split(jnp.concatenate([jnp.where(c == 0, own, other), jnp.where(c == 0, other, own)], axis=0))
        copies[g].wait()
        for p, cells in enumerate(planes_of(held_ref, g)):
            part = dot3(split(cells), both)
            out_ref[p] = part if g == 0 else out_ref[p] + part


def based(place, pieces, cells):
    sa, gx, own, planes, eight, width = cells.shape
    rank = pieces[0].shape[-1]
    wide = sa * own * eight
    return pl.pallas_call(
        based_kernel,
        in_specs=[SMEM] + [VMEM] * 4 + [HBM],
        out_specs=VMEM,
        out_shape=jax.ShapeDtypeStruct((planes, wide, rank), F32),
        scratch_shapes=held(cells),
        compiler_params=PARAMS,
        cost_estimate=cost(3 * 2 * planes * wide * gx * width * rank, 4 * (cells.size + planes * wide * rank)),
        name="field_times_basis_x",
    )(place, *pieces, pltpu.with_memory_space_constraint(cells, pltpu.HBM))


def mixing(factor, species, rank):
    low, wide = rank * 8, species * 8
    rep_r = (iota((low, rank), 0) // 8 == iota((low, rank), 1)).astype(F32)
    rep_s = (iota((species, wide), 0) == iota((species, wide), 1) // 8).astype(F32)
    mixed = exact(exact(rep_r, factor, NT), rep_s)
    same = (iota((low, wide), 0) % 8) == (iota((low, wide), 1) % 8)
    return split(jnp.where(same, mixed, 0.0))


def image_x_kernel(
    place_ref, grams_ref, basis_s_ref, based_ref, cells_ref, factor_ref, keep_ref, give_ref, hi_ref, lo_ref,
    held_ref, sems
):
    copies = bring(cells_ref, held_ref, sems)
    species, rank = basis_s_ref.shape
    planes, wide, columns = based_ref.shape
    image = exact(unfold(jnp.sum(grams_ref[...], axis=0), species // 2), basis_s_ref[...])
    factor = exact(image, invert_block(exact(image, image, TN)), NT)
    factor_ref[...] = factor
    mix = mixing(factor, species, rank)
    for p in range(planes):
        inner = split(dot3(mix, split(based_ref[p])))
        hi_ref[:, p * wide : (p + 1) * wide], lo_ref[:, p * wide : (p + 1) * wide] = split(dot3(inner, mix, TN))
    blocks = keep_ref.shape[0]
    for copy in copies:
        copy.wait()
    for image_ref, start in ((give_ref, (1 - place_ref[2]) * blocks), (keep_ref, place_ref[2] * blocks)):
        for i in range(blocks):
            cells = jnp.concatenate(planes_of(held_ref, start + i), axis=0)
            image_ref[i] = dot3((hi_ref[...], lo_ref[...]), split(cells))


def image_x_stage(place, grams, basis_s, product, cells):
    sa, gx, own, planes, eight, width = cells.shape
    columns = product.shape[2]
    half = jax.ShapeDtypeStruct((gx // 2, columns, width), F32)
    return pl.pallas_call(
        image_x_kernel,
        in_specs=[SMEM] + [VMEM] * 3 + [HBM],
        out_specs=[VMEM] * 3,
        out_shape=[jax.ShapeDtypeStruct(basis_s.shape, F32), half, half],
        scratch_shapes=[pltpu.VMEM((columns, planes * product.shape[1]), BF16)] * 2 + held(cells),
        compiler_params=PARAMS,
        name="factor_species_and_image_x",
    )(place, grams, basis_s, product, pltpu.with_memory_space_constraint(cells, pltpu.HBM))


def first_kernel(factor_ref, cells_ref, out_ref, hi_ref, lo_ref, held_ref, sems):
    copies = bring(cells_ref, held_ref, sems)
    species, rank = factor_ref.shape
    low = hi_ref.shape[0]
    hi_ref[...], lo_ref[...] = mixing(factor_ref[...], species, rank)
    for g in range(cells_ref.shape[1]):
        copies[g].wait()
        for p, cells in enumerate(planes_of(held_ref, g)):
            out_ref[g, p * low : (p + 1) * low, :] = dot3((hi_ref[...], lo_ref[...]), split(cells))


def first_stage(factor, cells):
    sa, gx, own, planes, eight, width = cells.shape
    species, rank = factor.shape
    low, wide = rank * 8, species * 8
    return pl.pallas_call(
        first_kernel,
        in_specs=[VMEM, HBM],
        out_specs=VMEM,
        out_shape=jax.ShapeDtypeStruct((gx, planes * low, width), F32),
        scratch_shapes=[pltpu.VMEM((low, wide), BF16)] * 2 + held(cells),
        compiler_params=PARAMS,
        cost_estimate=cost(3 * 2 * planes * low * wide * gx * width, 4 * (cells.size + gx * planes * low * width)),
        name="first",
    )(factor, pltpu.with_memory_space_constraint(cells, pltpu.HBM))


def second_kernel(place_ref, own_ref, other_ref, first_ref, factor_ref, send_ref, work_ref, hold_ref):
    half, rank, width = own_ref.shape
    gx, n = 2 * half, rank
    xl, y, c = place_ref[0], place_ref[1], place_ref[2]
    norms = jnp.zeros((n, n), F32)
    raw = jnp.zeros(hold_ref.shape, F32)
    for image_ref, start in ((own_ref, c * half), (other_ref, (1 - c) * half)):
        for i in range(half):
            norms += exact(image_ref[i], image_ref[i], NT)
            raw += dot3(split(first_ref[start + i]), split(image_ref[i]), NT)
    hold_ref[...] = raw
    fill(work_ref, norms)
    inverse = invert_factor(work_ref, n, 64)
    factor_ref[...] = exact(inverse, jnp.where(xl == c, own_ref[y], other_ref[y])).T
    second = exact(hold_ref[...], inverse, NT)
    hold_ref[...] = second
    groups = send_ref.shape[0] // gx
    each = 3
    lane = iota((8, 128), 1)
    for g in range(groups):
        for half in range(n // 128):
            tiles = [
                hold_ref[(g * each + j) * 8 : (g * each + j + 1) * 8, half * 128 : (half + 1) * 128]
                for j in range(each)
            ]
            for part in range(4):
                moved = [
                    tile if (j - part) % 4 == 0 else pltpu.roll(tile, ((j - part) % 4) * 32, 1)
                    for j, tile in enumerate(tiles)
                ]
                mixed = jnp.where(lane < 32, moved[0], jnp.where(lane < 64, moved[1], moved[2]))
                send_ref[g * gx + half * 4 + part] = jnp.where(lane < 96, mixed, 0.0)


def second_stage(place, own, other, first):
    half, rank, width = own.shape
    rows = first.shape[1]
    return pl.pallas_call(
        second_kernel,
        in_specs=[SMEM, VMEM, VMEM, VMEM],
        out_specs=[VMEM] * 2,
        out_shape=[
            jax.ShapeDtypeStruct((width, rank), F32),
            jax.ShapeDtypeStruct((rows // 24 * 2 * half, 8, 128), F32),
        ],
        scratch_shapes=[pltpu.VMEM((rank, 2 * rank), F32), pltpu.VMEM((rows, rank), F32)],
        compiler_params=PARAMS,
        name="factor_x_and_second",
    )(place, own, other, first)


def image_y_kernel(place_ref, near_ref, far_ref, near_o_ref, far_o_ref, second_ref, keep_ref, give_ref, basis_ref):
    xh, c, z = place_ref[3], place_ref[2], place_ref[4]
    count = near_ref.shape[0]
    for piece_ref, over, across in (
        (near_ref, xh, c), (far_ref, 1 - xh, c), (near_o_ref, xh, 1 - c), (far_o_ref, 1 - xh, 1 - c)
    ):
        for k in range(count):
            basis_ref[(over * 2 + across) * count + lax.rem(z + k, count)] = piece_ref[k]
    rows = second_ref.shape[0]
    turned = second_ref[...].T
    both = split(turned)
    inner = dot3(both, split(basis_ref[...].reshape(rows, basis_ref.shape[2])))
    left = split(inner.T)
    half, rank, width = keep_ref.shape
    for b in range(2 * half):
        cols = slice(b * width, (b + 1) * width)
        image = dot3(left, (both[0][:, cols], both[1][:, cols]))

        @pl.when(b // half == c)
        def _():
            keep_ref[b % half] = image

        @pl.when(b // half != c)
        def _():
            give_ref[b % half] = image


def image_y_stage(place, pieces, second):
    rank = pieces[0].shape[2]
    count, each = pieces[0].shape[:2]
    shape = jax.ShapeDtypeStruct((second.shape[0] // 512, rank, 256), F32)
    return pl.pallas_call(
        image_y_kernel,
        in_specs=[SMEM] + [VMEM] * 5,
        out_specs=[VMEM] * 2,
        out_shape=[shape, shape],
        scratch_shapes=[pltpu.VMEM((4 * count, each, rank), F32)],
        compiler_params=PARAMS,
        name="image_y",
    )(place, *pieces, second)


def core_kernel(place_ref, own_ref, other_ref, second_ref, factor_ref, core_ref, work_ref, turn_ref):
    half, n, width = own_ref.shape
    xh, c, z = place_ref[3], place_ref[2], place_ref[4]
    norms = jnp.zeros((n, n), F32)
    raw = jnp.zeros((n, second_ref.shape[1]), F32)
    for image_ref, start in ((own_ref, c * half), (other_ref, (1 - c) * half)):
        for b in range(half):
            image = image_ref[b]
            norms += exact(image, image, NT)
            first_row = pl.multiple_of((start + b) * width, width)
            raw += exact(image, second_ref[pl.ds(first_row, width), :])
    fill(work_ref, norms)
    inverse = invert_factor(work_ref, n, 64)
    core_ref[...] = exact(inverse, raw)
    turn_ref[...] = exact(inverse, jnp.where(xh == c, own_ref[c], other_ref[c])).T
    count = factor_ref.shape[0]
    factor_ref[...] = turn_ref[pl.ds(pl.multiple_of(z * count, count), count), :]


def core_stage(place, own, other, second, count):
    half, n, width = own.shape
    return pl.pallas_call(
        core_kernel,
        in_specs=[SMEM, VMEM, VMEM, VMEM],
        out_specs=[VMEM] * 2,
        out_shape=[
            jax.ShapeDtypeStruct((count, n), F32),
            jax.ShapeDtypeStruct((n, second.shape[1]), F32),
        ],
        scratch_shapes=[pltpu.VMEM((n, 2 * n), F32), pltpu.VMEM((width, n), F32)],
        compiler_params=PARAMS,
        name="factor_y_and_core",
    )(place, own, other, second)


def swap(parts, axes):
    return lax.all_to_all(parts, axes, split_axis=0, concat_axis=0, tiled=True)


def spread(one, axes, count):
    return swap(jnp.broadcast_to(one, (count,) + one.shape), axes)


def shifted(x, axis, count, by):
    return lax.ppermute(x, axis, [((i + by) % count, i) for i in range(count)])


def around(x, axis, count):
    return jnp.stack([x] + [shifted(x, axis, count, k) for k in range(1, count)])


def copies_kernel(parts_ref, out_ref):
    out_ref[...] = jnp.broadcast_to(jnp.sum(parts_ref[...], axis=0, keepdims=True), out_ref.shape)


def copies_of_sum(parts, count):
    return pl.pallas_call(
        copies_kernel,
        in_specs=[VMEM],
        out_specs=VMEM,
        out_shape=jax.ShapeDtypeStruct((count,) + parts.shape[1:], F32),
        compiler_params=PARAMS,
        name="copies_of_sum",
    )(parts)


def pair_kernel(one_ref, other_ref, out_ref):
    out_ref[...] = jnp.broadcast_to((one_ref[...] + other_ref[...])[None], out_ref.shape)


def copies_of_pair(one, other, count):
    return pl.pallas_call(
        pair_kernel,
        in_specs=[VMEM] * 2,
        out_specs=VMEM,
        out_shape=jax.ShapeDtypeStruct((count,) + one.shape, F32),
        compiler_params=PARAMS,
        name="copies_of_pair",
    )(one, other)


def after_kernel(x_ref, ready_ref, out_ref):
    del x_ref, ready_ref, out_ref


def after(x, ready):
    return pl.pallas_call(
        after_kernel,
        in_specs=[HBM, HBM],
        out_specs=HBM,
        out_shape=jax.ShapeDtypeStruct(x.shape, x.dtype),
        input_output_aliases={0: 0},
        compiler_params=PARAMS,
        name="after",
    )(x, ready)


def total(keep, give, beside=lambda mine: (mine, ())):
    mine = keep + shifted(give, "c", 2, 1)
    mine = copies_of_sum(swap(mine.reshape(64, mine.size // (64 * 256), 256), CHIPS), 64)
    mine, extra = beside(mine)
    own = swap(mine, CHIPS).reshape(keep.shape)
    return own, shifted(own, "c", 2, 1), extra


def local(field, basis_s, basis_x, basis_y):
    gx_n, sa_n = 8, 4
    place = jnp.stack([lax.axis_index(a) for a in ("xl", "y", "c", "xh", "z")])
    rows = basis_x.shape[0] // 2
    near_x = around(lax.dynamic_slice_in_dim(basis_x, lax.axis_index("c") * rows, rows, 0), "y", 4)
    packed, near_x = lax.optimization_barrier((pack(field, gx_n * sa_n), near_x))
    cells = swap(packed, ("z",) + GX)
    cells = cells.reshape((sa_n, gx_n) + cells.shape[1:])
    near_x, cells = lax.optimization_barrier((near_x, cells))
    far_x = shifted(near_x, "xl", 2, 1)
    partial = gram(cells)
    partial = copies_of_pair(partial, shifted(partial, "c", 2, 1), 64)
    far_x = after(far_x, partial)
    pieces_x = (near_x, far_x, shifted(near_x, "c", 2, 1), shifted(far_x, "c", 2, 1))
    grams = swap(partial, CHIPS)
    product = based(place, pieces_x, cells)
    factor_s, keep, give = image_x_stage(place, grams, basis_s, product, cells)
    give, late_y = lax.optimization_barrier((give, basis_y))
    first = first_stage(factor_s, cells)
    near_y = around(late_y, "z", 4)

    def beside(mine):
        mine, ready, near = lax.optimization_barrier((mine, first, near_y))
        return mine, (ready, near, shifted(near, "xh", 2, 1))

    own, other, (first, near_y, far_y) = total(keep, give, beside)
    factor_x, send = second_stage(place, own, other, first)
    second = swap(send, GY + ("z",) + GX).reshape(-1, 128)
    pieces_y = (near_y, far_y, shifted(near_y, "c", 2, 1), shifted(far_y, "c", 2, 1))
    own, other, _ = total(*image_y_stage(place, pieces_y, second))
    factor_y, core = core_stage(place, own, other, second, basis_y.shape[0])
    rank_y = core.shape[0]
    blocks = swap(core.reshape(16, rank_y // 16, 128), GY + ("z",))
    core = blocks.reshape(2, 8, rank_y // 16, 4, 32)[:, :, :, :3, :]
    core = core.transpose(2, 4, 1, 3, 0).reshape(rank_y // 16, 32, 24, 2)
    return core, factor_s, factor_x, factor_y


def solution(mesh):
    fine = Mesh(mesh.devices.reshape(2, 4, 2, 2, 4), ("xl", "y", "xh", "c", "z"))
    yz = GY + ("z",)
    return jax.shard_map(
        local,
        mesh=fine,
        in_specs=(P("z", None, GX, GY), P(), P(GX, None), P(yz, None)),
        out_specs=(P(yz, GX, None, None), P(), P(GX, None), P(yz, None)),
        check_vma=False,
    )
```

```python
import functools

import jax
import jax.numpy as jnp
from jax import lax
from jax.experimental import pallas as pl
from jax.experimental.pallas import tpu as pltpu
from jax.sharding import Mesh
from jax.sharding import PartitionSpec as P

F32 = jnp.float32
BF16 = jnp.bfloat16
HIGH = lax.Precision.HIGHEST
GX = ("xl", "y")
GY = ("xh", "c")
CHIPS = GX + ("xh", "z")
VMEM = pl.BlockSpec(memory_space=pltpu.VMEM)
SMEM = pl.BlockSpec(memory_space=pltpu.SMEM)
HBM = pl.BlockSpec(memory_space=pltpu.HBM)
PARAMS = pltpu.CompilerParams(vmem_limit_bytes=20 * 1024 * 1024)

NN = (((1,), (0,)), ((), ()))
NT = (((1,), (1,)), ((), ()))
TN = (((0,), (0,)), ((), ()))


def exact(a, b, dims=NN):
    return lax.dot_general(a, b, dims, precision=HIGH, preferred_element_type=F32)


def split(a):
    hi = a.astype(BF16)
    return hi, (a - hi.astype(F32)).astype(BF16)


def dot3(a, b, dims=NN):
    one = functools.partial(lax.dot_general, dimension_numbers=dims, preferred_element_type=F32)
    return one(a[0], b[0]) + (one(a[0], b[1]) + one(a[1], b[0]))


def iota(shape, dim):
    return lax.broadcasted_iota(jnp.int32, shape, dim)


def invert_block(block):
    n = block.shape[0]
    unit = (iota((n, n), 0) == iota((n, n), 1)).astype(F32)
    parts = [block, unit]
    if 2 * n < 128:
        parts.append(jnp.zeros((n, 128 - 2 * n), F32))
    work = jnp.concatenate(parts, axis=1)
    tiles = [work[i : i + 8, :] for i in range(0, n, 8)]
    full = (8, 128)
    sub = iota(full, 0)
    out = []
    for j, own in enumerate(tiles):
        rows = [jnp.broadcast_to(own[t : t + 1, :], full) for t in range(8)]
        columns = [
            [jnp.broadcast_to(tile[:, 8 * j + t : 8 * j + t + 1], full) for t in range(8)] for tile in tiles[j:]
        ]
        cells = {
            (t, u): jnp.broadcast_to(columns[0][u][t : t + 1, :], full) for t in range(8) for u in range(t, 8)
        }
        columns = columns[1:]
        done = jnp.zeros(full, F32)
        for t in range(8):
            inverse = 1.0 / cells[t, t]
            for u in range(t + 1, 8):
                share = cells[t, u] * inverse
                for v in range(u, 8):
                    cells[u, v] = cells[u, v] - share * cells[t, v]
                rows[u] = rows[u] - share * rows[t]
            for column in columns:
                share = column[t] * inverse
                for u in range(t + 1, 8):
                    column[u] = column[u] - share * cells[t, u]
                column[t] = share
            done = jnp.where(sub == t, rows[t] * lax.rsqrt(cells[t, t]), done)
        out.append(done)
        for i, column in enumerate(columns):
            tile = tiles[j + 1 + i]
            for t in range(8):
                tile = tile - column[t] * rows[t]
            tiles[j + 1 + i] = tile
    return jnp.concatenate(out, axis=0)[:, n : 2 * n]


def invert_factor(work_ref, n, size):
    for k in range(0, n, size):
        inner = invert_block(work_ref[k : k + size, k : k + size])
        row = exact(inner, work_ref[k : k + size, :])
        work_ref[k : k + size, :] = row
        if k + size < n:
            work_ref[k + size :, :] -= exact(row[:, k + size : n], row, TN)
    return work_ref[:, n:]


def fill(work_ref, norms):
    n = norms.shape[0]
    work_ref[:, :n] = norms
    work_ref[:, n:] = (iota((n, n), 0) == iota((n, n), 1)).astype(F32)


def pack_kernel(field_ref, out_ref, held_ref, turned_ref, in_sems, out_sems):
    species, planes, rows, cols = held_ref.shape
    coming = [pltpu.make_async_copy(field_ref.at[s], held_ref.at[s], in_sems.at[s]) for s in range(species)]
    going = [pltpu.make_async_copy(turned_ref.at[:, s], out_ref.at[:, s], out_sems.at[s]) for s in range(species)]
    for copy in coming:
        copy.start()
    for s in range(species):
        coming[s].wait()
        for p in range(planes):
            turned_ref[:, s, p] = held_ref[s, p].T.reshape(out_ref.shape[0], 8, rows)
        going[s].start()
    for copy in going:
        copy.wait()


def pack(field, groups):
    species, planes, rows, cols = field.shape
    shape = (groups, species, planes, 8, rows)
    return pl.pallas_call(
        pack_kernel,
        in_specs=[HBM],
        out_specs=HBM,
        out_shape=jax.ShapeDtypeStruct(shape, F32),
        scratch_shapes=[
            pltpu.VMEM(field.shape, F32),
            pltpu.VMEM(shape, F32),
            pltpu.SemaphoreType.DMA((species,)),
            pltpu.SemaphoreType.DMA((species,)),
        ],
        compiler_params=PARAMS,
        cost_estimate=cost(0, 8 * field.size),
        name="pack",
    )(pltpu.with_memory_space_constraint(field, pltpu.HBM))


def cost(flops, size):
    return pl.CostEstimate(flops=flops, bytes_accessed=size, transcendentals=0)


def bring(cells_ref, held_ref, sems):
    copies = [
        pltpu.make_async_copy(cells_ref.at[:, g], held_ref.at[:, g], sems.at[g]) for g in range(cells_ref.shape[1])
    ]
    for copy in copies:
        copy.start()
    return copies


def held(cells):
    return [pltpu.VMEM(cells.shape, F32), pltpu.SemaphoreType.DMA((cells.shape[1],))]


def planes_of(cells_ref, g):
    sa, gx, own, planes, eight, width = cells_ref.shape
    return [cells_ref[:, g, :, p].reshape(sa * own * eight, width) for p in range(planes)]


def gram_kernel(cells_ref, out_ref, acc_ref, held_ref, sems):
    copies = bring(cells_ref, held_ref, sems)
    count = acc_ref.shape[0]
    one = functools.partial(lax.dot_general, dimension_numbers=NT, preferred_element_type=F32)
    for g in range(cells_ref.shape[1]):
        copies[g].wait()
        hi, lo = split(jnp.concatenate(planes_of(held_ref, g), axis=1))
        twice = (lo.astype(F32) * 2.0).astype(BF16)
        part = one(hi, hi) + one(hi, twice)
        acc_ref[...] = part if g == 0 else acc_ref[...] + part
    same = (iota((count, count), 0) % 8) == (iota((count, count), 1) % 8)
    kept = jnp.where(same, acc_ref[...], 0.0)
    pick = (iota((count, 128), 0) // 8 == iota((count, 128), 1)).astype(F32)
    summed = exact(exact(pick, kept, TN), pick)
    both = 0.5 * (summed + summed.T)
    out_ref[...] = fold(both, count // 16)


def fold(both, half):
    row, lane = iota((half, 128), 0), iota((half, 128), 1)
    upper = both[:half, :]
    lower = pltpu.roll(both[half : 2 * half, :], 128 - half, 1)
    corner = jnp.where(row <= lane, upper, lower)
    full = jnp.where(lane < 2 * half, jnp.where(lane < half, corner, upper), 0.0)
    diagonal = jnp.sum(jnp.where(row == lane, lower, 0.0), axis=0, keepdims=True)
    rest = jnp.concatenate([full[16:half], jnp.broadcast_to(diagonal, (32 - half, 128))], axis=0)
    return full[:16] + pltpu.roll(rest, 64, 1)


def unfold(folded, half):
    rest = pltpu.roll(folded, 64, 1)
    full = jnp.concatenate([folded, rest[: half - 16]], axis=0)
    row, lane = iota((half, half), 0), iota((half, half), 1)
    corner, middle = full[:, :half], full[:, half : 2 * half]
    diagonal = jnp.broadcast_to(rest[half - 16 : half - 15, :half], (half, half))
    above = jnp.where(row <= lane, corner, 0.0)
    below = jnp.where(row > lane, corner, 0.0)
    first = above + jnp.where(row < lane, corner, 0.0).T
    last = below + below.T + jnp.where(row == lane, diagonal, 0.0)
    top = jnp.concatenate([first, middle], axis=1)
    return jnp.concatenate([top, jnp.concatenate([middle.T, last], axis=1)], axis=0)


def gram(cells):
    sa, gx, own, planes, eight, width = cells.shape
    species = sa * own
    return pl.pallas_call(
        gram_kernel,
        in_specs=[HBM],
        out_specs=VMEM,
        out_shape=jax.ShapeDtypeStruct((16, 128), F32),
        scratch_shapes=[pltpu.VMEM((species * 8, species * 8), F32)] + held(cells),
        compiler_params=PARAMS,
        cost_estimate=cost(4 * gx * planes * width * (8 * species) ** 2, 4 * cells.size),
        name="gram_species",
    )(pltpu.with_memory_space_constraint(cells, pltpu.HBM))


def based_kernel(place_ref, near_ref, far_ref, near_o_ref, far_o_ref, cells_ref, out_ref, held_ref, sems):
    xl, y, c = place_ref[0], place_ref[1], place_ref[2]
    quarter = near_ref.shape[0]
    copies = bring(cells_ref, held_ref, sems)
    for g in range(cells_ref.shape[1]):
        away = lax.rem(lax.rem(g, quarter) - y + quarter, quarter)
        here = g // quarter == xl
        own = jnp.where(here, near_ref[away], far_ref[away])
        other = jnp.where(here, near_o_ref[away], far_o_ref[away])
        both = split(jnp.concatenate([jnp.where(c == 0, own, other), jnp.where(c == 0, other, own)], axis=0))
        copies[g].wait()
        for p, cells in enumerate(planes_of(held_ref, g)):
            part = dot3(split(cells), both)
            out_ref[p] = part if g == 0 else out_ref[p] + part


def based(place, pieces, cells):
    sa, gx, own, planes, eight, width = cells.shape
    rank = pieces[0].shape[-1]
    wide = sa * own * eight
    return pl.pallas_call(
        based_kernel,
        in_specs=[SMEM] + [VMEM] * 4 + [HBM],
        out_specs=VMEM,
        out_shape=jax.ShapeDtypeStruct((planes, wide, rank), F32),
        scratch_shapes=held(cells),
        compiler_params=PARAMS,
        cost_estimate=cost(3 * 2 * planes * wide * gx * width * rank, 4 * (cells.size + planes * wide * rank)),
        name="field_times_basis_x",
    )(place, *pieces, pltpu.with_memory_space_constraint(cells, pltpu.HBM))


def mixing(factor, species, rank):
    low, wide = rank * 8, species * 8
    rep_r = (iota((low, rank), 0) // 8 == iota((low, rank), 1)).astype(F32)
    rep_s = (iota((species, wide), 0) == iota((species, wide), 1) // 8).astype(F32)
    mixed = exact(exact(rep_r, factor, NT), rep_s)
    same = (iota((low, wide), 0) % 8) == (iota((low, wide), 1) % 8)
    return split(jnp.where(same, mixed, 0.0))


def image_x_kernel(
    place_ref, grams_ref, basis_s_ref, based_ref, cells_ref, factor_ref, keep_ref, give_ref, hi_ref, lo_ref,
    held_ref, sems
):
    copies = bring(cells_ref, held_ref, sems)
    species, rank = basis_s_ref.shape
    planes, wide, columns = based_ref.shape
    image = exact(unfold(jnp.sum(grams_ref[...], axis=0), species // 2), basis_s_ref[...])
    factor = exact(image, invert_block(exact(image, image, TN)), NT)
    factor_ref[...] = factor
    mix = mixing(factor, species, rank)
    for p in range(planes):
        inner = split(dot3(mix, split(based_ref[p])))
        hi_ref[:, p * wide : (p + 1) * wide], lo_ref[:, p * wide : (p + 1) * wide] = split(dot3(inner, mix, TN))
    blocks = keep_ref.shape[0]
    for copy in copies:
        copy.wait()
    for image_ref, start in ((give_ref, (1 - place_ref[2]) * blocks), (keep_ref, place_ref[2] * blocks)):
        for i in range(blocks):
            cells = jnp.concatenate(planes_of(held_ref, start + i), axis=0)
            image_ref[i] = dot3((hi_ref[...], lo_ref[...]), split(cells))


def image_x_stage(place, grams, basis_s, product, cells):
    sa, gx, own, planes, eight, width = cells.shape
    columns = product.shape[2]
    half = jax.ShapeDtypeStruct((gx // 2, columns, width), F32)
    return pl.pallas_call(
        image_x_kernel,
        in_specs=[SMEM] + [VMEM] * 3 + [HBM],
        out_specs=[VMEM] * 3,
        out_shape=[jax.ShapeDtypeStruct(basis_s.shape, F32), half, half],
        scratch_shapes=[pltpu.VMEM((columns, planes * product.shape[1]), BF16)] * 2 + held(cells),
        compiler_params=PARAMS,
        name="factor_species_and_image_x",
    )(place, grams, basis_s, product, pltpu.with_memory_space_constraint(cells, pltpu.HBM))


def first_kernel(factor_ref, cells_ref, out_ref, hi_ref, lo_ref, held_ref, sems):
    copies = bring(cells_ref, held_ref, sems)
    species, rank = factor_ref.shape
    low = hi_ref.shape[0]
    hi_ref[...], lo_ref[...] = mixing(factor_ref[...], species, rank)
    for g in range(cells_ref.shape[1]):
        copies[g].wait()
        for p, cells in enumerate(planes_of(held_ref, g)):
            out_ref[g, p * low : (p + 1) * low, :] = dot3((hi_ref[...], lo_ref[...]), split(cells))


def first_stage(factor, cells):
    sa, gx, own, planes, eight, width = cells.shape
    species, rank = factor.shape
    low, wide = rank * 8, species * 8
    return pl.pallas_call(
        first_kernel,
        in_specs=[VMEM, HBM],
        out_specs=VMEM,
        out_shape=jax.ShapeDtypeStruct((gx, planes * low, width), F32),
        scratch_shapes=[pltpu.VMEM((low, wide), BF16)] * 2 + held(cells),
        compiler_params=PARAMS,
        cost_estimate=cost(3 * 2 * planes * low * wide * gx * width, 4 * (cells.size + gx * planes * low * width)),
        name="first",
    )(factor, pltpu.with_memory_space_constraint(cells, pltpu.HBM))


def products(image_ref, first_ref, start, norms, raw):
    for i in range(image_ref.shape[0]):
        norms += exact(image_ref[i], image_ref[i], NT)
        raw += dot3(split(first_ref[start + i]), split(image_ref[i]), NT)
    return norms, raw


def own_products_kernel(place_ref, own_ref, first_ref, norms_ref, raw_ref):
    zeros = jnp.zeros(norms_ref.shape, F32), jnp.zeros(raw_ref.shape, F32)
    norms_ref[...], raw_ref[...] = products(own_ref, first_ref, place_ref[2] * own_ref.shape[0], *zeros)


def own_products(place, own, first):
    half, rank, width = own.shape
    return pl.pallas_call(
        own_products_kernel,
        in_specs=[SMEM] + [VMEM] * 2,
        out_specs=[VMEM] * 2,
        out_shape=[
            jax.ShapeDtypeStruct((rank, rank), F32),
            jax.ShapeDtypeStruct((first.shape[1], rank), F32),
        ],
        compiler_params=PARAMS,
        cost_estimate=cost(2 * half * rank * width * (6 * rank + 3 * first.shape[1]), 4 * (own.size + first.size // 2)),
        name="own_products",
    )(place, own, first)


def second_kernel(place_ref, other_ref, first_ref, norms_ref, raw_ref, inverse_ref, send_ref, work_ref, hold_ref):
    half, n, width = other_ref.shape
    gx = 2 * half
    norms, raw = products(other_ref, first_ref, (1 - place_ref[2]) * half, norms_ref[...], raw_ref[...])
    hold_ref[...] = raw
    fill(work_ref, norms)
    inverse = invert_factor(work_ref, n, 64)
    inverse_ref[...] = inverse
    second = exact(hold_ref[...], inverse, NT)
    hold_ref[...] = second
    groups = send_ref.shape[0] // gx
    each = 3
    lane = iota((8, 128), 1)
    for g in range(groups):
        for half in range(n // 128):
            tiles = [
                hold_ref[(g * each + j) * 8 : (g * each + j + 1) * 8, half * 128 : (half + 1) * 128]
                for j in range(each)
            ]
            for part in range(4):
                moved = [
                    tile if (j - part) % 4 == 0 else pltpu.roll(tile, ((j - part) % 4) * 32, 1)
                    for j, tile in enumerate(tiles)
                ]
                mixed = jnp.where(lane < 32, moved[0], jnp.where(lane < 64, moved[1], moved[2]))
                send_ref[g * gx + half * 4 + part] = jnp.where(lane < 96, mixed, 0.0)


def second_stage(place, other, first, norms, raw):
    half, rank, width = other.shape
    rows = first.shape[1]
    return pl.pallas_call(
        second_kernel,
        in_specs=[SMEM] + [VMEM] * 4,
        out_specs=[VMEM] * 2,
        out_shape=[
            jax.ShapeDtypeStruct((rank, rank), F32),
            jax.ShapeDtypeStruct((rows // 24 * 2 * half, 8, 128), F32),
        ],
        scratch_shapes=[pltpu.VMEM((rank, 2 * rank), F32), pltpu.VMEM((rows, rank), F32)],
        compiler_params=PARAMS,
        name="inverse_x_and_second",
    )(place, other, first, norms, raw)


def factor_kernel(axes, place_ref, own_ref, other_ref, inverse_ref, out_ref, turn_ref):
    half_of, block_of, part_of = axes
    block = place_ref[block_of]
    image = jnp.where(place_ref[half_of] == place_ref[2], own_ref[block], other_ref[block])
    turn_ref[...] = exact(inverse_ref[...], image).T
    count = out_ref.shape[0]
    part = 0 if part_of is None else pl.multiple_of(place_ref[part_of] * count, count)
    out_ref[...] = turn_ref[pl.ds(part, count), :]


def factor_rows(axes, place, own, other, inverse, count):
    rank, width = own.shape[1:]
    return pl.pallas_call(
        functools.partial(factor_kernel, axes),
        in_specs=[SMEM] + [VMEM] * 3,
        out_specs=VMEM,
        out_shape=jax.ShapeDtypeStruct((count, rank), F32),
        scratch_shapes=[pltpu.VMEM((width, rank), F32)],
        compiler_params=PARAMS,
        cost_estimate=cost(12 * rank * rank * width, 4 * (3 * rank * width)),
        name="factor_rows",
    )(place, own, other, inverse)


def image_y_kernel(place_ref, near_ref, far_ref, near_o_ref, far_o_ref, second_ref, keep_ref, give_ref, basis_ref):
    xh, c, z = place_ref[3], place_ref[2], place_ref[4]
    count = near_ref.shape[0]
    for piece_ref, over, across in (
        (near_ref, xh, c), (far_ref, 1 - xh, c), (near_o_ref, xh, 1 - c), (far_o_ref, 1 - xh, 1 - c)
    ):
        for k in range(count):
            basis_ref[(over * 2 + across) * count + lax.rem(z + k, count)] = piece_ref[k]
    rows = second_ref.shape[0]
    turned = second_ref[...].T
    both = split(turned)
    inner = dot3(both, split(basis_ref[...].reshape(rows, basis_ref.shape[2])))
    left = split(inner.T)
    half, rank, width = keep_ref.shape
    for b in range(2 * half):
        cols = slice(b * width, (b + 1) * width)
        image = dot3(left, (both[0][:, cols], both[1][:, cols]))

        @pl.when(b // half == c)
        def _():
            keep_ref[b % half] = image

        @pl.when(b // half != c)
        def _():
            give_ref[b % half] = image


def image_y_stage(place, pieces, second):
    rank = pieces[0].shape[2]
    count, each = pieces[0].shape[:2]
    shape = jax.ShapeDtypeStruct((second.shape[0] // 512, rank, 256), F32)
    return pl.pallas_call(
        image_y_kernel,
        in_specs=[SMEM] + [VMEM] * 5,
        out_specs=[VMEM] * 2,
        out_shape=[shape, shape],
        scratch_shapes=[pltpu.VMEM((4 * count, each, rank), F32)],
        compiler_params=PARAMS,
        name="image_y",
    )(place, *pieces, second)


def core_kernel(place_ref, own_ref, other_ref, second_ref, inverse_ref, core_ref, work_ref):
    half, n, width = own_ref.shape
    c = place_ref[2]
    norms = jnp.zeros((n, n), F32)
    raw = jnp.zeros((n, second_ref.shape[1]), F32)
    for image_ref, start in ((own_ref, c * half), (other_ref, (1 - c) * half)):
        for b in range(half):
            image = image_ref[b]
            norms += exact(image, image, NT)
            first_row = pl.multiple_of((start + b) * width, width)
            raw += exact(image, second_ref[pl.ds(first_row, width), :])
    fill(work_ref, norms)
    inverse = invert_factor(work_ref, n, 64)
    inverse_ref[...] = inverse
    core_ref[...] = exact(inverse, raw)


def core_stage(place, own, other, second):
    half, n, width = own.shape
    return pl.pallas_call(
        core_kernel,
        in_specs=[SMEM, VMEM, VMEM, VMEM],
        out_specs=[VMEM] * 2,
        out_shape=[
            jax.ShapeDtypeStruct((n, n), F32),
            jax.ShapeDtypeStruct((n, second.shape[1]), F32),
        ],
        scratch_shapes=[pltpu.VMEM((n, 2 * n), F32)],
        compiler_params=PARAMS,
        name="inverse_y_and_core",
    )(place, own, other, second)


def swap(parts, axes):
    return lax.all_to_all(parts, axes, split_axis=0, concat_axis=0, tiled=True)


def spread(one, axes, count):
    return swap(jnp.broadcast_to(one, (count,) + one.shape), axes)


def shifted(x, axis, count, by):
    return lax.ppermute(x, axis, [((i + by) % count, i) for i in range(count)])


def around(x, axis, count):
    return jnp.stack([x] + [shifted(x, axis, count, k) for k in range(1, count)])


def copies_kernel(parts_ref, out_ref):
    out_ref[...] = jnp.broadcast_to(jnp.sum(parts_ref[...], axis=0, keepdims=True), out_ref.shape)


def copies_of_sum(parts, count):
    return pl.pallas_call(
        copies_kernel,
        in_specs=[VMEM],
        out_specs=VMEM,
        out_shape=jax.ShapeDtypeStruct((count,) + parts.shape[1:], F32),
        compiler_params=PARAMS,
        name="copies_of_sum",
    )(parts)


def pair_kernel(one_ref, other_ref, out_ref):
    out_ref[...] = jnp.broadcast_to((one_ref[...] + other_ref[...])[None], out_ref.shape)


def copies_of_pair(one, other, count):
    return pl.pallas_call(
        pair_kernel,
        in_specs=[VMEM] * 2,
        out_specs=VMEM,
        out_shape=jax.ShapeDtypeStruct((count,) + one.shape, F32),
        compiler_params=PARAMS,
        name="copies_of_pair",
    )(one, other)


def after_kernel(x_ref, ready_ref, out_ref):
    del x_ref, ready_ref, out_ref


def after(x, ready):
    return pl.pallas_call(
        after_kernel,
        in_specs=[HBM, HBM],
        out_specs=HBM,
        out_shape=jax.ShapeDtypeStruct(x.shape, x.dtype),
        input_output_aliases={0: 0},
        compiler_params=PARAMS,
        name="after",
    )(x, ready)


def total(keep, give, beside=lambda mine: (mine, ())):
    mine = keep + shifted(give, "c", 2, 1)
    mine = copies_of_sum(swap(mine.reshape(64, mine.size // (64 * 256), 256), CHIPS), 64)
    mine, extra = beside(mine)
    own = swap(mine, CHIPS).reshape(keep.shape)
    return own, shifted(own, "c", 2, 1), extra


def local(field, basis_s, basis_x, basis_y):
    gx_n, sa_n = 8, 4
    place = jnp.stack([lax.axis_index(a) for a in ("xl", "y", "c", "xh", "z")])
    rows = basis_x.shape[0] // 2
    near_x = around(lax.dynamic_slice_in_dim(basis_x, lax.axis_index("c") * rows, rows, 0), "y", 4)
    packed, near_x = lax.optimization_barrier((pack(field, gx_n * sa_n), near_x))
    cells = swap(packed, ("z",) + GX)
    cells = cells.reshape((sa_n, gx_n) + cells.shape[1:])
    near_x, cells = lax.optimization_barrier((near_x, cells))
    far_x = shifted(near_x, "xl", 2, 1)
    partial = gram(cells)
    partial = copies_of_pair(partial, shifted(partial, "c", 2, 1), 64)
    far_x = after(far_x, partial)
    pieces_x = (near_x, far_x, shifted(near_x, "c", 2, 1), shifted(far_x, "c", 2, 1))
    grams = swap(partial, CHIPS)
    product = based(place, pieces_x, cells)
    factor_s, keep, give = image_x_stage(place, grams, basis_s, product, cells)
    give, late_y = lax.optimization_barrier((give, basis_y))
    first = first_stage(factor_s, cells)
    near_y = around(late_y, "z", 4)

    def beside(mine):
        mine, ready, near = lax.optimization_barrier((mine, first, near_y))
        return mine, (ready, near, shifted(near, "xh", 2, 1))

    own, other, (first, near_y, far_y) = total(keep, give, beside)
    inverse_x, send = second_stage(place, other, first, *own_products(place, own, first))
    factor_x = factor_rows((0, 1, None), place, own, other, inverse_x, basis_x.shape[0])
    second = swap(send, GY + ("z",) + GX).reshape(-1, 128)
    pieces_y = (near_y, far_y, shifted(near_y, "c", 2, 1), shifted(far_y, "c", 2, 1))
    own, other, _ = total(*image_y_stage(place, pieces_y, second))
    inverse_y, core = core_stage(place, own, other, second)
    factor_y = factor_rows((3, 2, 4), place, own, other, inverse_y, basis_y.shape[0])
    rank_y = core.shape[0]
    blocks = swap(core.reshape(16, rank_y // 16, 128), GY + ("z",))
    core = blocks.reshape(2, 8, rank_y // 16, 4, 32)[:, :, :, :3, :]
    core = core.transpose(2, 4, 1, 3, 0).reshape(rank_y // 16, 32, 24, 2)
    return core, factor_s, factor_x, factor_y


def solution(mesh):
    fine = Mesh(mesh.devices.reshape(2, 4, 2, 2, 4), ("xl", "y", "xh", "c", "z"))
    yz = GY + ("z",)
    return jax.shard_map(
        local,
        mesh=fine,
        in_specs=(P("z", None, GX, GY), P(), P(GX, None), P(yz, None)),
        out_specs=(P(yz, GX, None, None), P(), P(GX, None), P(yz, None)),
        check_vma=False,
    )
```

```python
import functools

import jax
import jax.numpy as jnp
from jax import lax
from jax.experimental import pallas as pl
from jax.experimental.pallas import tpu as pltpu
from jax.sharding import Mesh
from jax.sharding import PartitionSpec as P

F32 = jnp.float32
BF16 = jnp.bfloat16
HIGH = lax.Precision.HIGHEST
GX = ("xl", "y")
GY = ("xh", "c")
CHIPS = GX + ("xh", "z")
VMEM = pl.BlockSpec(memory_space=pltpu.VMEM)
SMEM = pl.BlockSpec(memory_space=pltpu.SMEM)
HBM = pl.BlockSpec(memory_space=pltpu.HBM)
PARAMS = pltpu.CompilerParams(vmem_limit_bytes=20 * 1024 * 1024)

NN = (((1,), (0,)), ((), ()))
NT = (((1,), (1,)), ((), ()))
TN = (((0,), (0,)), ((), ()))


def exact(a, b, dims=NN):
    return lax.dot_general(a, b, dims, precision=HIGH, preferred_element_type=F32)


def split(a):
    hi = a.astype(BF16)
    return hi, (a - hi.astype(F32)).astype(BF16)


def dot3(a, b, dims=NN):
    one = functools.partial(lax.dot_general, dimension_numbers=dims, preferred_element_type=F32)
    return one(a[0], b[0]) + (one(a[0], b[1]) + one(a[1], b[0]))


def iota(shape, dim):
    return lax.broadcasted_iota(jnp.int32, shape, dim)


def invert_block(block):
    n = block.shape[0]
    unit = (iota((n, n), 0) == iota((n, n), 1)).astype(F32)
    parts = [block, unit]
    if 2 * n < 128:
        parts.append(jnp.zeros((n, 128 - 2 * n), F32))
    work = jnp.concatenate(parts, axis=1)
    tiles = [work[i : i + 8, :] for i in range(0, n, 8)]
    full = (8, 128)
    sub = iota(full, 0)
    out = []
    for j, own in enumerate(tiles):
        rows = [jnp.broadcast_to(own[t : t + 1, :], full) for t in range(8)]
        columns = [
            [jnp.broadcast_to(tile[:, 8 * j + t : 8 * j + t + 1], full) for t in range(8)] for tile in tiles[j:]
        ]
        cells = {
            (t, u): jnp.broadcast_to(columns[0][u][t : t + 1, :], full) for t in range(8) for u in range(t, 8)
        }
        columns = columns[1:]
        done = jnp.zeros(full, F32)
        for t in range(8):
            inverse = 1.0 / cells[t, t]
            for u in range(t + 1, 8):
                share = cells[t, u] * inverse
                for v in range(u, 8):
                    cells[u, v] = cells[u, v] - share * cells[t, v]
                rows[u] = rows[u] - share * rows[t]
            for column in columns:
                share = column[t] * inverse
                for u in range(t + 1, 8):
                    column[u] = column[u] - share * cells[t, u]
                column[t] = share
            done = jnp.where(sub == t, rows[t] * lax.rsqrt(cells[t, t]), done)
        out.append(done)
        for i, column in enumerate(columns):
            tile = tiles[j + 1 + i]
            for t in range(8):
                tile = tile - column[t] * rows[t]
            tiles[j + 1 + i] = tile
    return jnp.concatenate(out, axis=0)[:, n : 2 * n]


def invert_factor(work_ref, n, size):
    for k in range(0, n, size):
        inner = invert_block(work_ref[k : k + size, k : k + size])
        row = exact(inner, work_ref[k : k + size, :])
        work_ref[k : k + size, :] = row
        if k + size < n:
            work_ref[k + size :, :] -= exact(row[:, k + size : n], row, TN)
    return work_ref[:, n:]


def fill(work_ref, norms):
    n = norms.shape[0]
    work_ref[:, :n] = norms
    work_ref[:, n:] = (iota((n, n), 0) == iota((n, n), 1)).astype(F32)


def pack_kernel(plane, field_ref, out_ref, held_ref, turned_ref, in_sems, out_sems):
    species, rows, cols = held_ref.shape
    coming = [pltpu.make_async_copy(field_ref.at[s, plane], held_ref.at[s], in_sems.at[s]) for s in range(species)]
    going = [pltpu.make_async_copy(turned_ref.at[:, s], out_ref.at[:, s], out_sems.at[s]) for s in range(species)]
    for copy in coming:
        copy.start()
    for s in range(species):
        coming[s].wait()
        turned_ref[:, s] = held_ref[s].T.reshape(out_ref.shape[0], 8, rows)
        going[s].start()
    for copy in going:
        copy.wait()


def pack(field, plane, groups):
    species, planes, rows, cols = field.shape
    shape = (groups, species, 8, rows)
    return pl.pallas_call(
        functools.partial(pack_kernel, plane),
        in_specs=[HBM],
        out_specs=HBM,
        out_shape=jax.ShapeDtypeStruct(shape, F32),
        scratch_shapes=[
            pltpu.VMEM((species, rows, cols), F32),
            pltpu.VMEM(shape, F32),
            pltpu.SemaphoreType.DMA((species,)),
            pltpu.SemaphoreType.DMA((species,)),
        ],
        compiler_params=PARAMS,
        cost_estimate=cost(0, 4 * field.size),
        name="pack",
    )(pltpu.with_memory_space_constraint(field, pltpu.HBM))


def cost(flops, size):
    return pl.CostEstimate(flops=flops, bytes_accessed=size, transcendentals=0)


class Block:
    def __init__(self, copies):
        self.copies = copies
        for copy in copies:
            copy.start()

    def wait(self):
        for copy in self.copies:
            copy.wait()


def bring(cells_refs, held_ref, sems):
    return [
        Block(
            [
                pltpu.make_async_copy(ref.at[:, g], held_ref.at[:, g, :, p], sems.at[g, p])
                for p, ref in enumerate(cells_refs)
            ]
        )
        for g in range(held_ref.shape[1])
    ]


def held(cells):
    sa, gx, own, eight, width = cells[0].shape
    return [
        pltpu.VMEM((sa, gx, own, len(cells), eight, width), F32),
        pltpu.SemaphoreType.DMA((gx, len(cells))),
    ]


def pinned(cells):
    return [pltpu.with_memory_space_constraint(c, pltpu.HBM) for c in cells]


def planes_of(held_ref, g):
    sa, gx, own, planes, eight, width = held_ref.shape
    return [held_ref[:, g, :, p].reshape(sa * own * eight, width) for p in range(planes)]


def gram_kernel(cells_ref, before_ref, out_ref, acc_ref, held_ref, sems):
    copies = bring([cells_ref], held_ref, sems)
    count = acc_ref.shape[0]
    one = functools.partial(lax.dot_general, dimension_numbers=NT, preferred_element_type=F32)
    for g in range(held_ref.shape[1]):
        copies[g].wait()
        hi, lo = split(jnp.concatenate(planes_of(held_ref, g), axis=1))
        twice = (lo.astype(F32) * 2.0).astype(BF16)
        part = one(hi, hi) + one(hi, twice)
        acc_ref[...] = part if g == 0 else acc_ref[...] + part
    same = (iota((count, count), 0) % 8) == (iota((count, count), 1) % 8)
    kept = jnp.where(same, acc_ref[...], 0.0)
    pick = (iota((count, 128), 0) // 8 == iota((count, 128), 1)).astype(F32)
    summed = exact(exact(pick, kept, TN), pick)
    both = 0.5 * (summed + summed.T)
    out_ref[...] = before_ref[...] + fold(both, count // 16)


def fold(both, half):
    row, lane = iota((half, 128), 0), iota((half, 128), 1)
    upper = both[:half, :]
    lower = pltpu.roll(both[half : 2 * half, :], 128 - half, 1)
    corner = jnp.where(row <= lane, upper, lower)
    full = jnp.where(lane < 2 * half, jnp.where(lane < half, corner, upper), 0.0)
    diagonal = jnp.sum(jnp.where(row == lane, lower, 0.0), axis=0, keepdims=True)
    rest = jnp.concatenate([full[16:half], jnp.broadcast_to(diagonal, (32 - half, 128))], axis=0)
    return full[:16] + pltpu.roll(rest, 64, 1)


def unfold(folded, half):
    rest = pltpu.roll(folded, 64, 1)
    full = jnp.concatenate([folded, rest[: half - 16]], axis=0)
    row, lane = iota((half, half), 0), iota((half, half), 1)
    corner, middle = full[:, :half], full[:, half : 2 * half]
    diagonal = jnp.broadcast_to(rest[half - 16 : half - 15, :half], (half, half))
    above = jnp.where(row <= lane, corner, 0.0)
    below = jnp.where(row > lane, corner, 0.0)
    first = above + jnp.where(row < lane, corner, 0.0).T
    last = below + below.T + jnp.where(row == lane, diagonal, 0.0)
    top = jnp.concatenate([first, middle], axis=1)
    return jnp.concatenate([top, jnp.concatenate([middle.T, last], axis=1)], axis=0)


def gram(cells, before):
    sa, gx, own, eight, width = cells.shape
    species = sa * own
    return pl.pallas_call(
        gram_kernel,
        in_specs=[HBM, VMEM],
        out_specs=VMEM,
        out_shape=jax.ShapeDtypeStruct((16, 128), F32),
        scratch_shapes=[pltpu.VMEM((species * 8, species * 8), F32)] + held([cells]),
        compiler_params=PARAMS,
        cost_estimate=cost(4 * gx * width * (8 * species) ** 2, 4 * cells.size),
        name="gram_species",
    )(*pinned([cells]), before)


def based_kernel(place_ref, near_ref, far_ref, near_o_ref, far_o_ref, one_ref, two_ref, out_ref, held_ref, sems):
    xl, y, c = place_ref[0], place_ref[1], place_ref[2]
    quarter = near_ref.shape[0]
    copies = bring([one_ref, two_ref], held_ref, sems)
    for g in range(held_ref.shape[1]):
        away = lax.rem(lax.rem(g, quarter) - y + quarter, quarter)
        here = g // quarter == xl
        own = jnp.where(here, near_ref[away], far_ref[away])
        other = jnp.where(here, near_o_ref[away], far_o_ref[away])
        both = split(jnp.concatenate([jnp.where(c == 0, own, other), jnp.where(c == 0, other, own)], axis=0))
        copies[g].wait()
        for p, cells in enumerate(planes_of(held_ref, g)):
            part = dot3(split(cells), both)
            out_ref[p] = part if g == 0 else out_ref[p] + part


def based(place, pieces, cells):
    planes = len(cells)
    sa, gx, own, eight, width = cells[0].shape
    rank = pieces[0].shape[-1]
    wide = sa * own * eight
    return pl.pallas_call(
        based_kernel,
        in_specs=[SMEM] + [VMEM] * 4 + [HBM] * 2,
        out_specs=VMEM,
        out_shape=jax.ShapeDtypeStruct((planes, wide, rank), F32),
        scratch_shapes=held(cells),
        compiler_params=PARAMS,
        cost_estimate=cost(3 * 2 * planes * wide * gx * width * rank, 4 * (2 * cells[0].size + planes * wide * rank)),
        name="field_times_basis_x",
    )(place, *pieces, *pinned(cells))


def mixing(factor, species, rank):
    low, wide = rank * 8, species * 8
    rep_r = (iota((low, rank), 0) // 8 == iota((low, rank), 1)).astype(F32)
    rep_s = (iota((species, wide), 0) == iota((species, wide), 1) // 8).astype(F32)
    mixed = exact(exact(rep_r, factor, NT), rep_s)
    same = (iota((low, wide), 0) % 8) == (iota((low, wide), 1) % 8)
    return split(jnp.where(same, mixed, 0.0))


def image_x_kernel(
    place_ref, grams_ref, basis_s_ref, based_ref, one_ref, two_ref, factor_ref, keep_ref, give_ref, hi_ref, lo_ref,
    held_ref, sems
):
    copies = bring([one_ref, two_ref], held_ref, sems)
    species, rank = basis_s_ref.shape
    planes, wide, columns = based_ref.shape
    image = exact(unfold(jnp.sum(grams_ref[...], axis=0), species // 2), basis_s_ref[...])
    factor = exact(image, invert_block(exact(image, image, TN)), NT)
    factor_ref[...] = factor
    mix = mixing(factor, species, rank)
    for p in range(planes):
        inner = split(dot3(mix, split(based_ref[p])))
        hi_ref[:, p * wide : (p + 1) * wide], lo_ref[:, p * wide : (p + 1) * wide] = split(dot3(inner, mix, TN))
    blocks = keep_ref.shape[0]
    for copy in copies:
        copy.wait()
    for image_ref, start in ((give_ref, (1 - place_ref[2]) * blocks), (keep_ref, place_ref[2] * blocks)):
        for i in range(blocks):
            cells = jnp.concatenate(planes_of(held_ref, start + i), axis=0)
            image_ref[i] = dot3((hi_ref[...], lo_ref[...]), split(cells))


def image_x_stage(place, grams, basis_s, product, cells):
    planes = len(cells)
    sa, gx, own, eight, width = cells[0].shape
    columns = product.shape[2]
    half = jax.ShapeDtypeStruct((gx // 2, columns, width), F32)
    return pl.pallas_call(
        image_x_kernel,
        in_specs=[SMEM] + [VMEM] * 3 + [HBM] * 2,
        out_specs=[VMEM] * 3,
        out_shape=[jax.ShapeDtypeStruct(basis_s.shape, F32), half, half],
        scratch_shapes=[pltpu.VMEM((columns, planes * product.shape[1]), BF16)] * 2 + held(cells),
        compiler_params=PARAMS,
        name="factor_species_and_image_x",
    )(place, grams, basis_s, product, *pinned(cells))


def first_kernel(factor_ref, one_ref, two_ref, out_ref, hi_ref, lo_ref, held_ref, sems):
    copies = bring([one_ref, two_ref], held_ref, sems)
    species, rank = factor_ref.shape
    low = hi_ref.shape[0]
    hi_ref[...], lo_ref[...] = mixing(factor_ref[...], species, rank)
    for g in range(held_ref.shape[1]):
        copies[g].wait()
        for p, cells in enumerate(planes_of(held_ref, g)):
            out_ref[g, p * low : (p + 1) * low, :] = dot3((hi_ref[...], lo_ref[...]), split(cells))


def first_stage(factor, cells):
    planes = len(cells)
    sa, gx, own, eight, width = cells[0].shape
    species, rank = factor.shape
    low, wide = rank * 8, species * 8
    return pl.pallas_call(
        first_kernel,
        in_specs=[VMEM] + [HBM] * 2,
        out_specs=VMEM,
        out_shape=jax.ShapeDtypeStruct((gx, planes * low, width), F32),
        scratch_shapes=[pltpu.VMEM((low, wide), BF16)] * 2 + held(cells),
        compiler_params=PARAMS,
        cost_estimate=cost(3 * 2 * planes * low * wide * gx * width, 4 * (2 * cells[0].size + gx * planes * low * width)),
        name="first",
    )(factor, *pinned(cells))


def second_kernel(place_ref, own_ref, other_ref, first_ref, factor_ref, send_ref, work_ref, hold_ref):
    half, rank, width = own_ref.shape
    gx, n = 2 * half, rank
    xl, y, c = place_ref[0], place_ref[1], place_ref[2]
    norms = jnp.zeros((n, n), F32)
    raw = jnp.zeros(hold_ref.shape, F32)
    for image_ref, start in ((own_ref, c * half), (other_ref, (1 - c) * half)):
        for i in range(half):
            norms += exact(image_ref[i], image_ref[i], NT)
            raw += dot3(split(first_ref[start + i]), split(image_ref[i]), NT)
    hold_ref[...] = raw
    fill(work_ref, norms)
    inverse = invert_factor(work_ref, n, 64)
    factor_ref[...] = exact(inverse, jnp.where(xl == c, own_ref[y], other_ref[y])).T
    second = exact(hold_ref[...], inverse, NT)
    hold_ref[...] = second
    groups = send_ref.shape[0] // gx
    each = 3
    lane = iota((8, 128), 1)
    for g in range(groups):
        for half in range(n // 128):
            tiles = [
                hold_ref[(g * each + j) * 8 : (g * each + j + 1) * 8, half * 128 : (half + 1) * 128]
                for j in range(each)
            ]
            for part in range(4):
                moved = [
                    tile if (j - part) % 4 == 0 else pltpu.roll(tile, ((j - part) % 4) * 32, 1)
                    for j, tile in enumerate(tiles)
                ]
                mixed = jnp.where(lane < 32, moved[0], jnp.where(lane < 64, moved[1], moved[2]))
                send_ref[g * gx + half * 4 + part] = jnp.where(lane < 96, mixed, 0.0)


def second_stage(place, own, other, first):
    half, rank, width = own.shape
    rows = first.shape[1]
    return pl.pallas_call(
        second_kernel,
        in_specs=[SMEM, VMEM, VMEM, VMEM],
        out_specs=[VMEM] * 2,
        out_shape=[
            jax.ShapeDtypeStruct((width, rank), F32),
            jax.ShapeDtypeStruct((rows // 24 * 2 * half, 8, 128), F32),
        ],
        scratch_shapes=[pltpu.VMEM((rank, 2 * rank), F32), pltpu.VMEM((rows, rank), F32)],
        compiler_params=PARAMS,
        name="factor_x_and_second",
    )(place, own, other, first)


def image_y_kernel(place_ref, near_ref, far_ref, near_o_ref, far_o_ref, second_ref, keep_ref, give_ref, basis_ref):
    xh, c, z = place_ref[3], place_ref[2], place_ref[4]
    count = near_ref.shape[0]
    for piece_ref, over, across in (
        (near_ref, xh, c), (far_ref, 1 - xh, c), (near_o_ref, xh, 1 - c), (far_o_ref, 1 - xh, 1 - c)
    ):
        for k in range(count):
            basis_ref[(over * 2 + across) * count + lax.rem(z + k, count)] = piece_ref[k]
    rows = second_ref.shape[0]
    turned = second_ref[...].T
    both = split(turned)
    inner = dot3(both, split(basis_ref[...].reshape(rows, basis_ref.shape[2])))
    left = split(inner.T)
    half, rank, width = keep_ref.shape
    for b in range(2 * half):
        cols = slice(b * width, (b + 1) * width)
        image = dot3(left, (both[0][:, cols], both[1][:, cols]))

        @pl.when(b // half == c)
        def _():
            keep_ref[b % half] = image

        @pl.when(b // half != c)
        def _():
            give_ref[b % half] = image


def image_y_stage(place, pieces, second):
    rank = pieces[0].shape[2]
    count, each = pieces[0].shape[:2]
    shape = jax.ShapeDtypeStruct((second.shape[0] // 512, rank, 256), F32)
    return pl.pallas_call(
        image_y_kernel,
        in_specs=[SMEM] + [VMEM] * 5,
        out_specs=[VMEM] * 2,
        out_shape=[shape, shape],
        scratch_shapes=[pltpu.VMEM((4 * count, each, rank), F32)],
        compiler_params=PARAMS,
        name="image_y",
    )(place, *pieces, second)


def core_kernel(place_ref, own_ref, other_ref, second_ref, factor_ref, core_ref, work_ref, turn_ref):
    half, n, width = own_ref.shape
    xh, c, z = place_ref[3], place_ref[2], place_ref[4]
    norms = jnp.zeros((n, n), F32)
    raw = jnp.zeros((n, second_ref.shape[1]), F32)
    for image_ref, start in ((own_ref, c * half), (other_ref, (1 - c) * half)):
        for b in range(half):
            image = image_ref[b]
            norms += exact(image, image, NT)
            first_row = pl.multiple_of((start + b) * width, width)
            raw += exact(image, second_ref[pl.ds(first_row, width), :])
    fill(work_ref, norms)
    inverse = invert_factor(work_ref, n, 64)
    core_ref[...] = exact(inverse, raw)
    turn_ref[...] = exact(inverse, jnp.where(xh == c, own_ref[c], other_ref[c])).T
    count = factor_ref.shape[0]
    factor_ref[...] = turn_ref[pl.ds(pl.multiple_of(z * count, count), count), :]


def core_stage(place, own, other, second, count):
    half, n, width = own.shape
    return pl.pallas_call(
        core_kernel,
        in_specs=[SMEM, VMEM, VMEM, VMEM],
        out_specs=[VMEM] * 2,
        out_shape=[
            jax.ShapeDtypeStruct((count, n), F32),
            jax.ShapeDtypeStruct((n, second.shape[1]), F32),
        ],
        scratch_shapes=[pltpu.VMEM((n, 2 * n), F32), pltpu.VMEM((width, n), F32)],
        compiler_params=PARAMS,
        name="factor_y_and_core",
    )(place, own, other, second)


def swap(parts, axes):
    return lax.all_to_all(parts, axes, split_axis=0, concat_axis=0, tiled=True)


def spread(one, axes, count):
    return swap(jnp.broadcast_to(one, (count,) + one.shape), axes)


def shifted(x, axis, count, by):
    return lax.ppermute(x, axis, [((i + by) % count, i) for i in range(count)])


def around(x, axis, count):
    return jnp.stack([x] + [shifted(x, axis, count, k) for k in range(1, count)])


def copies_kernel(parts_ref, out_ref):
    out_ref[...] = jnp.broadcast_to(jnp.sum(parts_ref[...], axis=0, keepdims=True), out_ref.shape)


def copies_of_sum(parts, count):
    return pl.pallas_call(
        copies_kernel,
        in_specs=[VMEM],
        out_specs=VMEM,
        out_shape=jax.ShapeDtypeStruct((count,) + parts.shape[1:], F32),
        compiler_params=PARAMS,
        name="copies_of_sum",
    )(parts)


def pair_kernel(one_ref, other_ref, out_ref):
    out_ref[...] = jnp.broadcast_to((one_ref[...] + other_ref[...])[None], out_ref.shape)


def copies_of_pair(one, other, count):
    return pl.pallas_call(
        pair_kernel,
        in_specs=[VMEM] * 2,
        out_specs=VMEM,
        out_shape=jax.ShapeDtypeStruct((count,) + one.shape, F32),
        compiler_params=PARAMS,
        name="copies_of_pair",
    )(one, other)


def after_kernel(x_ref, ready_ref, out_ref):
    del x_ref, ready_ref, out_ref


def after(x, ready):
    return pl.pallas_call(
        after_kernel,
        in_specs=[HBM, HBM],
        out_specs=HBM,
        out_shape=jax.ShapeDtypeStruct(x.shape, x.dtype),
        input_output_aliases={0: 0},
        compiler_params=PARAMS,
        name="after",
    )(x, ready)


def total(keep, give, beside=lambda mine: (mine, ())):
    mine = keep + shifted(give, "c", 2, 1)
    mine = copies_of_sum(swap(mine.reshape(64, mine.size // (64 * 256), 256), CHIPS), 64)
    mine, extra = beside(mine)
    own = swap(mine, CHIPS).reshape(keep.shape)
    return own, shifted(own, "c", 2, 1), extra


def local(field, basis_s, basis_x, basis_y):
    gx_n, sa_n = 8, 4
    place = jnp.stack([lax.axis_index(a) for a in ("xl", "y", "c", "xh", "z")])
    rows = basis_x.shape[0] // 2
    near_x = around(lax.dynamic_slice_in_dim(basis_x, lax.axis_index("c") * rows, rows, 0), "y", 4)
    packed, near_x = lax.optimization_barrier((pack(field, 0, gx_n * sa_n), near_x))
    cells = []
    for part in (packed, pack(field, 1, gx_n * sa_n)):
        part = swap(part, ("z",) + GX)
        cells.append(part.reshape((sa_n, gx_n) + part.shape[1:]))
    near_x, cells[1] = lax.optimization_barrier((near_x, cells[1]))
    far_x = shifted(near_x, "xl", 2, 1)
    partial = gram(cells[1], gram(cells[0], jnp.zeros((16, 128), F32)))
    partial = copies_of_pair(partial, shifted(partial, "c", 2, 1), 64)
    far_x = after(far_x, partial)
    pieces_x = (near_x, far_x, shifted(near_x, "c", 2, 1), shifted(far_x, "c", 2, 1))
    grams = swap(partial, CHIPS)
    product = based(place, pieces_x, cells)
    factor_s, keep, give = image_x_stage(place, grams, basis_s, product, cells)
    give, late_y = lax.optimization_barrier((give, basis_y))
    first = first_stage(factor_s, cells)
    near_y = around(late_y, "z", 4)

    def beside(mine):
        mine, ready, near = lax.optimization_barrier((mine, first, near_y))
        return mine, (ready, near, shifted(near, "xh", 2, 1))

    own, other, (first, near_y, far_y) = total(keep, give, beside)
    factor_x, send = second_stage(place, own, other, first)
    second = swap(send, GY + ("z",) + GX).reshape(-1, 128)
    pieces_y = (near_y, far_y, shifted(near_y, "c", 2, 1), shifted(far_y, "c", 2, 1))
    own, other, _ = total(*image_y_stage(place, pieces_y, second))
    factor_y, core = core_stage(place, own, other, second, basis_y.shape[0])
    rank_y = core.shape[0]
    blocks = swap(core.reshape(16, rank_y // 16, 128), GY + ("z",))
    core = blocks.reshape(2, 8, rank_y // 16, 4, 32)[:, :, :, :3, :]
    core = core.transpose(2, 4, 1, 3, 0).reshape(rank_y // 16, 32, 24, 2)
    return core, factor_s, factor_x, factor_y


def solution(mesh):
    fine = Mesh(mesh.devices.reshape(2, 4, 2, 2, 4), ("xl", "y", "xh", "c", "z"))
    yz = GY + ("z",)
    return jax.shard_map(
        local,
        mesh=fine,
        in_specs=(P("z", None, GX, GY), P(), P(GX, None), P(yz, None)),
        out_specs=(P(yz, GX, None, None), P(), P(GX, None), P(yz, None)),
        check_vma=False,
    )
```

```python
import functools

import jax
import jax.numpy as jnp
from jax import lax
from jax.experimental import pallas as pl
from jax.experimental.pallas import tpu as pltpu
from jax.sharding import Mesh
from jax.sharding import PartitionSpec as P

F32 = jnp.float32
BF16 = jnp.bfloat16
HIGH = lax.Precision.HIGHEST
GX = ("xl", "y")
GY = ("xh", "c")
CHIPS = GX + ("xh", "z")
VMEM = pl.BlockSpec(memory_space=pltpu.VMEM)
SMEM = pl.BlockSpec(memory_space=pltpu.SMEM)
HBM = pl.BlockSpec(memory_space=pltpu.HBM)
PARAMS = pltpu.CompilerParams(vmem_limit_bytes=20 * 1024 * 1024)

NN = (((1,), (0,)), ((), ()))
NT = (((1,), (1,)), ((), ()))
TN = (((0,), (0,)), ((), ()))


def exact(a, b, dims=NN):
    return lax.dot_general(a, b, dims, precision=HIGH, preferred_element_type=F32)


def split(a):
    hi = a.astype(BF16)
    return hi, (a - hi.astype(F32)).astype(BF16)


def dot3(a, b, dims=NN):
    one = functools.partial(lax.dot_general, dimension_numbers=dims, preferred_element_type=F32)
    return one(a[0], b[0]) + (one(a[0], b[1]) + one(a[1], b[0]))


def iota(shape, dim):
    return lax.broadcasted_iota(jnp.int32, shape, dim)


def invert_block(block):
    n = block.shape[0]
    unit = (iota((n, n), 0) == iota((n, n), 1)).astype(F32)
    parts = [block, unit]
    if 2 * n < 128:
        parts.append(jnp.zeros((n, 128 - 2 * n), F32))
    work = jnp.concatenate(parts, axis=1)
    tiles = [work[i : i + 8, :] for i in range(0, n, 8)]
    full = (8, 128)
    sub = iota(full, 0)
    out = []
    for j, own in enumerate(tiles):
        rows = [jnp.broadcast_to(own[t : t + 1, :], full) for t in range(8)]
        columns = [
            [jnp.broadcast_to(tile[:, 8 * j + t : 8 * j + t + 1], full) for t in range(8)] for tile in tiles[j:]
        ]
        cells = {
            (t, u): jnp.broadcast_to(columns[0][u][t : t + 1, :], full) for t in range(8) for u in range(t, 8)
        }
        columns = columns[1:]
        done = jnp.zeros(full, F32)
        for t in range(8):
            inverse = 1.0 / cells[t, t]
            for u in range(t + 1, 8):
                share = cells[t, u] * inverse
                for v in range(u, 8):
                    cells[u, v] = cells[u, v] - share * cells[t, v]
                rows[u] = rows[u] - share * rows[t]
            for column in columns:
                share = column[t] * inverse
                for u in range(t + 1, 8):
                    column[u] = column[u] - share * cells[t, u]
                column[t] = share
            done = jnp.where(sub == t, rows[t] * lax.rsqrt(cells[t, t]), done)
        out.append(done)
        for i, column in enumerate(columns):
            tile = tiles[j + 1 + i]
            for t in range(8):
                tile = tile - column[t] * rows[t]
            tiles[j + 1 + i] = tile
    return jnp.concatenate(out, axis=0)[:, n : 2 * n]


def invert_factor(work_ref, n, size):
    for k in range(0, n, size):
        inner = invert_block(work_ref[k : k + size, k : k + size])
        row = exact(inner, work_ref[k : k + size, :])
        work_ref[k : k + size, :] = row
        if k + size < n:
            work_ref[k + size :, :] -= exact(row[:, k + size : n], row, TN)
    return work_ref[:, n:]


def fill(work_ref, norms):
    n = norms.shape[0]
    work_ref[:, :n] = norms
    work_ref[:, n:] = (iota((n, n), 0) == iota((n, n), 1)).astype(F32)


def pack_kernel(field_ref, out_ref, held_ref, turned_ref, in_sems, out_sems):
    species, planes, rows, cols = held_ref.shape
    coming = [pltpu.make_async_copy(field_ref.at[s], held_ref.at[s], in_sems.at[s]) for s in range(species)]
    going = [pltpu.make_async_copy(turned_ref.at[:, s], out_ref.at[:, s], out_sems.at[s]) for s in range(species)]
    for copy in coming:
        copy.start()
    for s in range(species):
        coming[s].wait()
        for p in range(planes):
            turned_ref[:, s, p] = held_ref[s, p].T.reshape(out_ref.shape[0], 8, rows)
        going[s].start()
    for copy in going:
        copy.wait()


def pack(field, groups):
    species, planes, rows, cols = field.shape
    shape = (groups, species, planes, 8, rows)
    return pl.pallas_call(
        pack_kernel,
        in_specs=[HBM],
        out_specs=HBM,
        out_shape=jax.ShapeDtypeStruct(shape, F32),
        scratch_shapes=[
            pltpu.VMEM(field.shape, F32),
            pltpu.VMEM(shape, F32),
            pltpu.SemaphoreType.DMA((species,)),
            pltpu.SemaphoreType.DMA((species,)),
        ],
        compiler_params=PARAMS,
        cost_estimate=cost(0, 8 * field.size),
        name="pack",
    )(pltpu.with_memory_space_constraint(field, pltpu.HBM))


def cost(flops, size):
    return pl.CostEstimate(flops=flops, bytes_accessed=size, transcendentals=0)


class Block:
    def __init__(self, copies):
        self.copies = copies
        for copy in copies:
            copy.start()

    def wait(self):
        for copy in self.copies:
            copy.wait()


def bring(cells_ref, held_ref, sems):
    sa, gx = cells_ref.shape[:2]
    return [
        Block([pltpu.make_async_copy(cells_ref.at[z, g], held_ref.at[z, g], sems.at[g, z]) for z in range(sa)])
        for g in range(gx)
    ]


def held(cells):
    return [pltpu.VMEM(cells.shape, F32), pltpu.SemaphoreType.DMA((cells.shape[1], cells.shape[0]))]


def planes_of(cells_ref, g):
    sa, gx, own, planes, eight, width = cells_ref.shape
    return [cells_ref[:, g, :, p].reshape(sa * own * eight, width) for p in range(planes)]


def gram_kernel(cells_ref, out_ref, acc_ref, held_ref, sems):
    copies = bring(cells_ref, held_ref, sems)
    count = acc_ref.shape[0]
    one = functools.partial(lax.dot_general, dimension_numbers=NT, preferred_element_type=F32)
    for g in range(cells_ref.shape[1]):
        copies[g].wait()
        hi, lo = split(jnp.concatenate(planes_of(held_ref, g), axis=1))
        twice = (lo.astype(F32) * 2.0).astype(BF16)
        part = one(hi, hi) + one(hi, twice)
        acc_ref[...] = part if g == 0 else acc_ref[...] + part
    same = (iota((count, count), 0) % 8) == (iota((count, count), 1) % 8)
    kept = jnp.where(same, acc_ref[...], 0.0)
    pick = (iota((count, 128), 0) // 8 == iota((count, 128), 1)).astype(F32)
    summed = exact(exact(pick, kept, TN), pick)
    both = 0.5 * (summed + summed.T)
    out_ref[...] = fold(both, count // 16)


def fold(both, half):
    row, lane = iota((half, 128), 0), iota((half, 128), 1)
    upper = both[:half, :]
    lower = pltpu.roll(both[half : 2 * half, :], 128 - half, 1)
    corner = jnp.where(row <= lane, upper, lower)
    full = jnp.where(lane < 2 * half, jnp.where(lane < half, corner, upper), 0.0)
    diagonal = jnp.sum(jnp.where(row == lane, lower, 0.0), axis=0, keepdims=True)
    rest = jnp.concatenate([full[16:half], jnp.broadcast_to(diagonal, (32 - half, 128))], axis=0)
    return full[:16] + pltpu.roll(rest, 64, 1)


def unfold(folded, half):
    rest = pltpu.roll(folded, 64, 1)
    full = jnp.concatenate([folded, rest[: half - 16]], axis=0)
    row, lane = iota((half, half), 0), iota((half, half), 1)
    corner, middle = full[:, :half], full[:, half : 2 * half]
    diagonal = jnp.broadcast_to(rest[half - 16 : half - 15, :half], (half, half))
    above = jnp.where(row <= lane, corner, 0.0)
    below = jnp.where(row > lane, corner, 0.0)
    first = above + jnp.where(row < lane, corner, 0.0).T
    last = below + below.T + jnp.where(row == lane, diagonal, 0.0)
    top = jnp.concatenate([first, middle], axis=1)
    return jnp.concatenate([top, jnp.concatenate([middle.T, last], axis=1)], axis=0)


def gram(cells):
    sa, gx, own, planes, eight, width = cells.shape
    species = sa * own
    return pl.pallas_call(
        gram_kernel,
        in_specs=[HBM],
        out_specs=VMEM,
        out_shape=jax.ShapeDtypeStruct((16, 128), F32),
        scratch_shapes=[pltpu.VMEM((species * 8, species * 8), F32)] + held(cells),
        compiler_params=PARAMS,
        cost_estimate=cost(4 * gx * planes * width * (8 * species) ** 2, 4 * cells.size),
        name="gram_species",
    )(pltpu.with_memory_space_constraint(cells, pltpu.HBM))


def based_kernel(place_ref, near_ref, far_ref, near_o_ref, far_o_ref, cells_ref, out_ref, held_ref, sems):
    xl, y, c = place_ref[0], place_ref[1], place_ref[2]
    quarter = near_ref.shape[0]
    copies = bring(cells_ref, held_ref, sems)
    for g in range(cells_ref.shape[1]):
        away = lax.rem(lax.rem(g, quarter) - y + quarter, quarter)
        here = g // quarter == xl
        own = jnp.where(here, near_ref[away], far_ref[away])
        other = jnp.where(here, near_o_ref[away], far_o_ref[away])
        both = split(jnp.concatenate([jnp.where(c == 0, own, other), jnp.where(c == 0, other, own)], axis=0))
        copies[g].wait()
        for p, cells in enumerate(planes_of(held_ref, g)):
            part = dot3(split(cells), both)
            out_ref[p] = part if g == 0 else out_ref[p] + part


def based(place, pieces, cells):
    sa, gx, own, planes, eight, width = cells.shape
    rank = pieces[0].shape[-1]
    wide = sa * own * eight
    return pl.pallas_call(
        based_kernel,
        in_specs=[SMEM] + [VMEM] * 4 + [HBM],
        out_specs=VMEM,
        out_shape=jax.ShapeDtypeStruct((planes, wide, rank), F32),
        scratch_shapes=held(cells),
        compiler_params=PARAMS,
        cost_estimate=cost(3 * 2 * planes * wide * gx * width * rank, 4 * (cells.size + planes * wide * rank)),
        name="field_times_basis_x",
    )(place, *pieces, pltpu.with_memory_space_constraint(cells, pltpu.HBM))


def mixing(factor, species, rank):
    low, wide = rank * 8, species * 8
    rep_s = (iota((species, wide), 0) == iota((species, wide), 1) // 8).astype(F32)
    mixed = jnp.broadcast_to(exact(factor, rep_s, TN)[:, None, :], (rank, 8, wide)).reshape(low, wide)
    same = (iota((low, wide), 0) % 8) == (iota((low, wide), 1) % 8)
    return split(jnp.where(same, mixed, 0.0))


def image_x_kernel(
    place_ref, grams_ref, basis_s_ref, based_ref, cells_ref, factor_ref, keep_ref, give_ref, hi_ref, lo_ref,
    held_ref, sems
):
    copies = bring(cells_ref, held_ref, sems)
    species, rank = basis_s_ref.shape
    planes, wide, columns = based_ref.shape
    image = exact(unfold(jnp.sum(grams_ref[...], axis=0), species // 2), basis_s_ref[...])
    factor = exact(image, invert_block(exact(image, image, TN)), NT)
    factor_ref[...] = factor
    mix = mixing(factor, species, rank)
    for p in range(planes):
        inner = split(dot3(mix, split(based_ref[p])))
        hi_ref[:, p * wide : (p + 1) * wide], lo_ref[:, p * wide : (p + 1) * wide] = split(dot3(inner, mix, TN))
    blocks = keep_ref.shape[0]
    for copy in copies:
        copy.wait()
    for image_ref, start in ((give_ref, (1 - place_ref[2]) * blocks), (keep_ref, place_ref[2] * blocks)):
        for i in range(blocks):
            cells = jnp.concatenate(planes_of(held_ref, start + i), axis=0)
            image_ref[i] = dot3((hi_ref[...], lo_ref[...]), split(cells))


def image_x_stage(place, grams, basis_s, product, cells):
    sa, gx, own, planes, eight, width = cells.shape
    columns = product.shape[2]
    half = jax.ShapeDtypeStruct((gx // 2, columns, width), F32)
    return pl.pallas_call(
        image_x_kernel,
        in_specs=[SMEM] + [VMEM] * 3 + [HBM],
        out_specs=[VMEM] * 3,
        out_shape=[jax.ShapeDtypeStruct(basis_s.shape, F32), half, half],
        scratch_shapes=[pltpu.VMEM((columns, planes * product.shape[1]), BF16)] * 2 + held(cells),
        compiler_params=PARAMS,
        name="factor_species_and_image_x",
    )(place, grams, basis_s, product, pltpu.with_memory_space_constraint(cells, pltpu.HBM))


def first_kernel(factor_ref, cells_ref, out_ref, hi_ref, lo_ref, held_ref, sems):
    copies = bring(cells_ref, held_ref, sems)
    species, rank = factor_ref.shape
    low = hi_ref.shape[0]
    hi_ref[...], lo_ref[...] = mixing(factor_ref[...], species, rank)
    for g in range(cells_ref.shape[1]):
        copies[g].wait()
        for p, cells in enumerate(planes_of(held_ref, g)):
            out_ref[g, p * low : (p + 1) * low, :] = dot3((hi_ref[...], lo_ref[...]), split(cells))


def first_stage(factor, cells):
    sa, gx, own, planes, eight, width = cells.shape
    species, rank = factor.shape
    low, wide = rank * 8, species * 8
    return pl.pallas_call(
        first_kernel,
        in_specs=[VMEM, HBM],
        out_specs=VMEM,
        out_shape=jax.ShapeDtypeStruct((gx, planes * low, width), F32),
        scratch_shapes=[pltpu.VMEM((low, wide), BF16)] * 2 + held(cells),
        compiler_params=PARAMS,
        cost_estimate=cost(3 * 2 * planes * low * wide * gx * width, 4 * (cells.size + gx * planes * low * width)),
        name="first",
    )(factor, pltpu.with_memory_space_constraint(cells, pltpu.HBM))


def second_kernel(place_ref, own_ref, other_ref, first_ref, factor_ref, send_ref, work_ref, hold_ref):
    half, rank, width = own_ref.shape
    gx, n = 2 * half, rank
    xl, y, c = place_ref[0], place_ref[1], place_ref[2]
    norms = jnp.zeros((n, n), F32)
    raw = jnp.zeros(hold_ref.shape, F32)
    for image_ref, start in ((own_ref, c * half), (other_ref, (1 - c) * half)):
        for i in range(half):
            norms += exact(image_ref[i], image_ref[i], NT)
            raw += dot3(split(first_ref[start + i]), split(image_ref[i]), NT)
    hold_ref[...] = raw
    fill(work_ref, norms)
    inverse = invert_factor(work_ref, n, 64)
    factor_ref[...] = exact(inverse, jnp.where(xl == c, own_ref[y], other_ref[y])).T
    second = exact(hold_ref[...], inverse, NT)
    hold_ref[...] = second
    groups = send_ref.shape[0] // gx
    each = 3
    lane = iota((8, 128), 1)
    for g in range(groups):
        for half in range(n // 128):
            tiles = [
                hold_ref[(g * each + j) * 8 : (g * each + j + 1) * 8, half * 128 : (half + 1) * 128]
                for j in range(each)
            ]
            for part in range(4):
                moved = [
                    tile if (j - part) % 4 == 0 else pltpu.roll(tile, ((j - part) % 4) * 32, 1)
                    for j, tile in enumerate(tiles)
                ]
                mixed = jnp.where(lane < 32, moved[0], jnp.where(lane < 64, moved[1], moved[2]))
                send_ref[g * gx + half * 4 + part] = jnp.where(lane < 96, mixed, 0.0)


def second_stage(place, own, other, first):
    half, rank, width = own.shape
    rows = first.shape[1]
    return pl.pallas_call(
        second_kernel,
        in_specs=[SMEM, VMEM, VMEM, VMEM],
        out_specs=[VMEM] * 2,
        out_shape=[
            jax.ShapeDtypeStruct((width, rank), F32),
            jax.ShapeDtypeStruct((rows // 24 * 2 * half, 8, 128), F32),
        ],
        scratch_shapes=[pltpu.VMEM((rank, 2 * rank), F32), pltpu.VMEM((rows, rank), F32)],
        compiler_params=PARAMS,
        name="factor_x_and_second",
    )(place, own, other, first)


def image_y_kernel(place_ref, near_ref, far_ref, near_o_ref, far_o_ref, second_ref, keep_ref, give_ref, basis_ref):
    xh, c, z = place_ref[3], place_ref[2], place_ref[4]
    count = near_ref.shape[0]
    for piece_ref, over, across in (
        (near_ref, xh, c), (far_ref, 1 - xh, c), (near_o_ref, xh, 1 - c), (far_o_ref, 1 - xh, 1 - c)
    ):
        for k in range(count):
            basis_ref[(over * 2 + across) * count + lax.rem(z + k, count)] = piece_ref[k]
    rows = second_ref.shape[0]
    turned = second_ref[...].T
    both = split(turned)
    inner = dot3(both, split(basis_ref[...].reshape(rows, basis_ref.shape[2])))
    left = split(inner.T)
    half, rank, width = keep_ref.shape
    for b in range(2 * half):
        cols = slice(b * width, (b + 1) * width)
        image = dot3(left, (both[0][:, cols], both[1][:, cols]))

        @pl.when(b // half == c)
        def _():
            keep_ref[b % half] = image

        @pl.when(b // half != c)
        def _():
            give_ref[b % half] = image


def image_y_stage(place, pieces, second):
    rank = pieces[0].shape[2]
    count, each = pieces[0].shape[:2]
    shape = jax.ShapeDtypeStruct((second.shape[0] // 512, rank, 256), F32)
    return pl.pallas_call(
        image_y_kernel,
        in_specs=[SMEM] + [VMEM] * 5,
        out_specs=[VMEM] * 2,
        out_shape=[shape, shape],
        scratch_shapes=[pltpu.VMEM((4 * count, each, rank), F32)],
        compiler_params=PARAMS,
        name="image_y",
    )(place, *pieces, second)


def core_kernel(place_ref, own_ref, other_ref, second_ref, factor_ref, core_ref, work_ref, turn_ref):
    half, n, width = own_ref.shape
    xh, c, z = place_ref[3], place_ref[2], place_ref[4]
    norms = jnp.zeros((n, n), F32)
    raw = jnp.zeros((n, second_ref.shape[1]), F32)
    for image_ref, start in ((own_ref, c * half), (other_ref, (1 - c) * half)):
        for b in range(half):
            image = image_ref[b]
            norms += exact(image, image, NT)
            first_row = pl.multiple_of((start + b) * width, width)
            raw += exact(image, second_ref[pl.ds(first_row, width), :])
    fill(work_ref, norms)
    inverse = invert_factor(work_ref, n, 64)
    core_ref[...] = exact(inverse, raw)
    turn_ref[...] = exact(inverse, jnp.where(xh == c, own_ref[c], other_ref[c])).T
    count = factor_ref.shape[0]
    factor_ref[...] = turn_ref[pl.ds(pl.multiple_of(z * count, count), count), :]


def core_stage(place, own, other, second, count):
    half, n, width = own.shape
    return pl.pallas_call(
        core_kernel,
        in_specs=[SMEM, VMEM, VMEM, VMEM],
        out_specs=[VMEM] * 2,
        out_shape=[
            jax.ShapeDtypeStruct((count, n), F32),
            jax.ShapeDtypeStruct((n, second.shape[1]), F32),
        ],
        scratch_shapes=[pltpu.VMEM((n, 2 * n), F32), pltpu.VMEM((width, n), F32)],
        compiler_params=PARAMS,
        name="factor_y_and_core",
    )(place, own, other, second)


def swap(parts, axes):
    return lax.all_to_all(parts, axes, split_axis=0, concat_axis=0, tiled=True)


def spread(one, axes, count):
    return swap(jnp.broadcast_to(one, (count,) + one.shape), axes)


def shifted(x, axis, count, by):
    return lax.ppermute(x, axis, [((i + by) % count, i) for i in range(count)])


def around(x, axis, count):
    return jnp.stack([x] + [shifted(x, axis, count, k) for k in range(1, count)])


def copies_kernel(parts_ref, out_ref):
    out_ref[...] = jnp.broadcast_to(jnp.sum(parts_ref[...], axis=0, keepdims=True), out_ref.shape)


def copies_of_sum(parts, count):
    return pl.pallas_call(
        copies_kernel,
        in_specs=[VMEM],
        out_specs=VMEM,
        out_shape=jax.ShapeDtypeStruct((count,) + parts.shape[1:], F32),
        compiler_params=PARAMS,
        name="copies_of_sum",
    )(parts)


def pair_kernel(one_ref, other_ref, out_ref):
    out_ref[...] = jnp.broadcast_to((one_ref[...] + other_ref[...])[None], out_ref.shape)


def copies_of_pair(one, other, count):
    return pl.pallas_call(
        pair_kernel,
        in_specs=[VMEM] * 2,
        out_specs=VMEM,
        out_shape=jax.ShapeDtypeStruct((count,) + one.shape, F32),
        compiler_params=PARAMS,
        name="copies_of_pair",
    )(one, other)


def after_kernel(x_ref, ready_ref, out_ref):
    del x_ref, ready_ref, out_ref


def after(x, ready):
    return pl.pallas_call(
        after_kernel,
        in_specs=[HBM, HBM],
        out_specs=HBM,
        out_shape=jax.ShapeDtypeStruct(x.shape, x.dtype),
        input_output_aliases={0: 0},
        compiler_params=PARAMS,
        name="after",
    )(x, ready)


def total(keep, give, beside=lambda mine: (mine, ())):
    mine = keep + shifted(give, "c", 2, 1)
    mine = copies_of_sum(swap(mine.reshape(64, mine.size // (64 * 256), 256), CHIPS), 64)
    mine, extra = beside(mine)
    own = swap(mine, CHIPS).reshape(keep.shape)
    return own, shifted(own, "c", 2, 1), extra


def local(field, basis_s, basis_x, basis_y):
    gx_n, sa_n = 8, 4
    place = jnp.stack([lax.axis_index(a) for a in ("xl", "y", "c", "xh", "z")])
    rows = basis_x.shape[0] // 2
    near_x = around(lax.dynamic_slice_in_dim(basis_x, lax.axis_index("c") * rows, rows, 0), "y", 4)
    packed, near_x = lax.optimization_barrier((pack(field, gx_n * sa_n), near_x))
    cells = swap(packed, ("z",) + GX)
    cells = cells.reshape((sa_n, gx_n) + cells.shape[1:])
    near_x, cells = lax.optimization_barrier((near_x, cells))
    far_x = shifted(near_x, "xl", 2, 1)
    partial = gram(cells)
    partial = copies_of_pair(partial, shifted(partial, "c", 2, 1), 64)
    far_x = after(far_x, partial)
    pieces_x = (near_x, far_x, shifted(near_x, "c", 2, 1), shifted(far_x, "c", 2, 1))
    grams = swap(partial, CHIPS)
    product = based(place, pieces_x, cells)
    factor_s, keep, give = image_x_stage(place, grams, basis_s, product, cells)
    give, late_y = lax.optimization_barrier((give, basis_y))
    first = first_stage(factor_s, cells)
    near_y = around(late_y, "z", 4)

    def beside(mine):
        mine, ready, near = lax.optimization_barrier((mine, first, near_y))
        return mine, (ready, near, shifted(near, "xh", 2, 1))

    own, other, (first, near_y, far_y) = total(keep, give, beside)
    factor_x, send = second_stage(place, own, other, first)
    second = swap(send, GY + ("z",) + GX).reshape(-1, 128)
    pieces_y = (near_y, far_y, shifted(near_y, "c", 2, 1), shifted(far_y, "c", 2, 1))
    own, other, _ = total(*image_y_stage(place, pieces_y, second))
    factor_y, core = core_stage(place, own, other, second, basis_y.shape[0])
    rank_y = core.shape[0]
    blocks = swap(core.reshape(16, rank_y // 16, 128), GY + ("z",))
    core = blocks.reshape(2, 8, rank_y // 16, 4, 32)[:, :, :, :3, :]
    core = core.transpose(2, 4, 1, 3, 0).reshape(rank_y // 16, 32, 24, 2)
    return core, factor_s, factor_x, factor_y


def solution(mesh):
    fine = Mesh(mesh.devices.reshape(2, 4, 2, 2, 4), ("xl", "y", "xh", "c", "z"))
    yz = GY + ("z",)
    return jax.shard_map(
        local,
        mesh=fine,
        in_specs=(P("z", None, GX, GY), P(), P(GX, None), P(yz, None)),
        out_specs=(P(yz, GX, None, None), P(), P(GX, None), P(yz, None)),
        check_vma=False,
    )
```

```python
import functools

import jax
import jax.numpy as jnp
from jax import lax
from jax.experimental import pallas as pl
from jax.experimental.pallas import tpu as pltpu
from jax.sharding import Mesh
from jax.sharding import PartitionSpec as P

F32 = jnp.float32
BF16 = jnp.bfloat16
HIGH = lax.Precision.HIGHEST
GX = ("xl", "y")
GY = ("xh", "c")
CHIPS = GX + ("xh", "z")
VMEM = pl.BlockSpec(memory_space=pltpu.VMEM)
SMEM = pl.BlockSpec(memory_space=pltpu.SMEM)
HBM = pl.BlockSpec(memory_space=pltpu.HBM)
PARAMS = pltpu.CompilerParams(vmem_limit_bytes=20 * 1024 * 1024)

NN = (((1,), (0,)), ((), ()))
NT = (((1,), (1,)), ((), ()))
TN = (((0,), (0,)), ((), ()))


def exact(a, b, dims=NN):
    return lax.dot_general(a, b, dims, precision=HIGH, preferred_element_type=F32)


def split(a):
    hi = a.astype(BF16)
    return hi, (a - hi.astype(F32)).astype(BF16)


def dot3(a, b, dims=NN):
    one = functools.partial(lax.dot_general, dimension_numbers=dims, preferred_element_type=F32)
    return one(a[0], b[0]) + (one(a[0], b[1]) + one(a[1], b[0]))


def iota(shape, dim):
    return lax.broadcasted_iota(jnp.int32, shape, dim)


def invert_block(block):
    n = block.shape[0]
    unit = (iota((n, n), 0) == iota((n, n), 1)).astype(F32)
    parts = [block, unit]
    if 2 * n < 128:
        parts.append(jnp.zeros((n, 128 - 2 * n), F32))
    work = jnp.concatenate(parts, axis=1)
    tiles = [work[i : i + 8, :] for i in range(0, n, 8)]
    full = (8, 128)
    sub = iota(full, 0)
    out = []
    for j, own in enumerate(tiles):
        rows = [jnp.broadcast_to(own[t : t + 1, :], full) for t in range(8)]
        columns = [
            [jnp.broadcast_to(tile[:, 8 * j + t : 8 * j + t + 1], full) for t in range(8)] for tile in tiles[j:]
        ]
        cells = {
            (t, u): jnp.broadcast_to(columns[0][u][t : t + 1, :], full) for t in range(8) for u in range(t, 8)
        }
        columns = columns[1:]
        done = jnp.zeros(full, F32)
        for t in range(8):
            inverse = 1.0 / cells[t, t]
            for u in range(t + 1, 8):
                share = cells[t, u] * inverse
                for v in range(u, 8):
                    cells[u, v] = cells[u, v] - share * cells[t, v]
                rows[u] = rows[u] - share * rows[t]
            for column in columns:
                share = column[t] * inverse
                for u in range(t + 1, 8):
                    column[u] = column[u] - share * cells[t, u]
                column[t] = share
            done = jnp.where(sub == t, rows[t] * lax.rsqrt(cells[t, t]), done)
        out.append(done)
        for i, column in enumerate(columns):
            tile = tiles[j + 1 + i]
            for t in range(8):
                tile = tile - column[t] * rows[t]
            tiles[j + 1 + i] = tile
    return jnp.concatenate(out, axis=0)[:, n : 2 * n]


def invert_factor(work_ref, n, size):
    for k in range(0, n, size):
        inner = invert_block(work_ref[k : k + size, k : k + size])
        row = exact(inner, work_ref[k : k + size, :])
        work_ref[k : k + size, :] = row
        if k + size < n:
            work_ref[k + size :, :] -= exact(row[:, k + size : n], row, TN)
    return work_ref[:, n:]


def fill(work_ref, norms):
    n = norms.shape[0]
    work_ref[:, :n] = norms
    work_ref[:, n:] = (iota((n, n), 0) == iota((n, n), 1)).astype(F32)


def pack_kernel(field_ref, out_ref, held_ref, turned_ref, in_sems, out_sems):
    species, planes, rows, cols = held_ref.shape
    coming = [pltpu.make_async_copy(field_ref.at[s], held_ref.at[s], in_sems.at[s]) for s in range(species)]
    going = [pltpu.make_async_copy(turned_ref.at[:, :, s], out_ref.at[:, :, s], out_sems.at[s]) for s in range(species)]
    for copy in coming:
        copy.start()
    for s in range(species):
        coming[s].wait()
        for p in range(planes):
            turned_ref[:, p, s] = held_ref[s, p].T.reshape(out_ref.shape[0], 8, rows)
        going[s].start()
    for copy in going:
        copy.wait()


def pack(field, groups):
    species, planes, rows, cols = field.shape
    shape = (groups, planes, species, 8, rows)
    return pl.pallas_call(
        pack_kernel,
        in_specs=[HBM],
        out_specs=HBM,
        out_shape=jax.ShapeDtypeStruct(shape, F32),
        scratch_shapes=[
            pltpu.VMEM(field.shape, F32),
            pltpu.VMEM(shape, F32),
            pltpu.SemaphoreType.DMA((species,)),
            pltpu.SemaphoreType.DMA((species,)),
        ],
        compiler_params=PARAMS,
        cost_estimate=cost(0, 8 * field.size),
        name="pack",
    )(pltpu.with_memory_space_constraint(field, pltpu.HBM))


def cost(flops, size):
    return pl.CostEstimate(flops=flops, bytes_accessed=size, transcendentals=0)


class Block:
    def __init__(self, copies):
        self.copies = copies
        for copy in copies:
            copy.start()

    def wait(self):
        for copy in self.copies:
            copy.wait()


def bring(cells_ref, held_ref, sems):
    gx, planes = cells_ref.shape[1:3]
    return [
        Block([pltpu.make_async_copy(cells_ref.at[:, g, p], held_ref.at[:, g, p], sems.at[g, p]) for p in range(planes)])
        for g in range(gx)
    ]


def held(cells):
    return [pltpu.VMEM(cells.shape, F32), pltpu.SemaphoreType.DMA(cells.shape[1:3])]


def planes_of(cells_ref, g):
    sa, gx, planes, own, eight, width = cells_ref.shape
    return [cells_ref[:, g, p].reshape(sa * own * eight, width) for p in range(planes)]


def gram_kernel(cells_ref, out_ref, acc_ref, held_ref, sems):
    copies = bring(cells_ref, held_ref, sems)
    count = acc_ref.shape[0]
    one = functools.partial(lax.dot_general, dimension_numbers=NT, preferred_element_type=F32)
    for g in range(cells_ref.shape[1]):
        copies[g].wait()
        hi, lo = split(jnp.concatenate(planes_of(held_ref, g), axis=1))
        twice = (lo.astype(F32) * 2.0).astype(BF16)
        part = one(hi, hi) + one(hi, twice)
        acc_ref[...] = part if g == 0 else acc_ref[...] + part
    same = (iota((count, count), 0) % 8) == (iota((count, count), 1) % 8)
    kept = jnp.where(same, acc_ref[...], 0.0)
    pick = (iota((count, 128), 0) // 8 == iota((count, 128), 1)).astype(F32)
    summed = exact(exact(pick, kept, TN), pick)
    both = 0.5 * (summed + summed.T)
    out_ref[...] = fold(both, count // 16)


def fold(both, half):
    row, lane = iota((half, 128), 0), iota((half, 128), 1)
    upper = both[:half, :]
    lower = pltpu.roll(both[half : 2 * half, :], 128 - half, 1)
    corner = jnp.where(row <= lane, upper, lower)
    full = jnp.where(lane < 2 * half, jnp.where(lane < half, corner, upper), 0.0)
    diagonal = jnp.sum(jnp.where(row == lane, lower, 0.0), axis=0, keepdims=True)
    rest = jnp.concatenate([full[16:half], jnp.broadcast_to(diagonal, (32 - half, 128))], axis=0)
    return full[:16] + pltpu.roll(rest, 64, 1)


def unfold(folded, half):
    rest = pltpu.roll(folded, 64, 1)
    full = jnp.concatenate([folded, rest[: half - 16]], axis=0)
    row, lane = iota((half, half), 0), iota((half, half), 1)
    corner, middle = full[:, :half], full[:, half : 2 * half]
    diagonal = jnp.broadcast_to(rest[half - 16 : half - 15, :half], (half, half))
    above = jnp.where(row <= lane, corner, 0.0)
    below = jnp.where(row > lane, corner, 0.0)
    first = above + jnp.where(row < lane, corner, 0.0).T
    last = below + below.T + jnp.where(row == lane, diagonal, 0.0)
    top = jnp.concatenate([first, middle], axis=1)
    return jnp.concatenate([top, jnp.concatenate([middle.T, last], axis=1)], axis=0)


def gram(cells):
    sa, gx, planes, own, eight, width = cells.shape
    species = sa * own
    return pl.pallas_call(
        gram_kernel,
        in_specs=[HBM],
        out_specs=VMEM,
        out_shape=jax.ShapeDtypeStruct((16, 128), F32),
        scratch_shapes=[pltpu.VMEM((species * 8, species * 8), F32)] + held(cells),
        compiler_params=PARAMS,
        cost_estimate=cost(4 * gx * planes * width * (8 * species) ** 2, 4 * cells.size),
        name="gram_species",
    )(pltpu.with_memory_space_constraint(cells, pltpu.HBM))


def based_kernel(place_ref, near_ref, far_ref, near_o_ref, far_o_ref, cells_ref, out_ref, held_ref, sems):
    xl, y, c = place_ref[0], place_ref[1], place_ref[2]
    quarter = near_ref.shape[0]
    copies = bring(cells_ref, held_ref, sems)
    for g in range(cells_ref.shape[1]):
        away = lax.rem(lax.rem(g, quarter) - y + quarter, quarter)
        here = g // quarter == xl
        own = jnp.where(here, near_ref[away], far_ref[away])
        other = jnp.where(here, near_o_ref[away], far_o_ref[away])
        both = split(jnp.concatenate([jnp.where(c == 0, own, other), jnp.where(c == 0, other, own)], axis=0))
        copies[g].wait()
        for p, cells in enumerate(planes_of(held_ref, g)):
            part = dot3(split(cells), both)
            out_ref[p] = part if g == 0 else out_ref[p] + part


def based(place, pieces, cells):
    sa, gx, planes, own, eight, width = cells.shape
    rank = pieces[0].shape[-1]
    wide = sa * own * eight
    return pl.pallas_call(
        based_kernel,
        in_specs=[SMEM] + [VMEM] * 4 + [HBM],
        out_specs=VMEM,
        out_shape=jax.ShapeDtypeStruct((planes, wide, rank), F32),
        scratch_shapes=held(cells),
        compiler_params=PARAMS,
        cost_estimate=cost(3 * 2 * planes * wide * gx * width * rank, 4 * (cells.size + planes * wide * rank)),
        name="field_times_basis_x",
    )(place, *pieces, pltpu.with_memory_space_constraint(cells, pltpu.HBM))


def mixing(factor, species, rank):
    low, wide = rank * 8, species * 8
    rep_s = (iota((species, wide), 0) == iota((species, wide), 1) // 8).astype(F32)
    mixed = jnp.broadcast_to(exact(factor, rep_s, TN)[:, None, :], (rank, 8, wide)).reshape(low, wide)
    same = (iota((low, wide), 0) % 8) == (iota((low, wide), 1) % 8)
    return split(jnp.where(same, mixed, 0.0))


def image_x_kernel(
    place_ref, grams_ref, basis_s_ref, based_ref, cells_ref, factor_ref, keep_ref, give_ref, hi_ref, lo_ref,
    held_ref, sems
):
    copies = bring(cells_ref, held_ref, sems)
    species, rank = basis_s_ref.shape
    planes, wide, columns = based_ref.shape
    image = exact(unfold(jnp.sum(grams_ref[...], axis=0), species // 2), basis_s_ref[...])
    factor = exact(image, invert_block(exact(image, image, TN)), NT)
    factor_ref[...] = factor
    mix = mixing(factor, species, rank)
    for p in range(planes):
        inner = split(dot3(mix, split(based_ref[p])))
        hi_ref[:, p * wide : (p + 1) * wide], lo_ref[:, p * wide : (p + 1) * wide] = split(dot3(inner, mix, TN))
    blocks = keep_ref.shape[0]
    for copy in copies:
        copy.wait()
    for image_ref, start in ((give_ref, (1 - place_ref[2]) * blocks), (keep_ref, place_ref[2] * blocks)):
        for i in range(blocks):
            cells = jnp.concatenate(planes_of(held_ref, start + i), axis=0)
            image_ref[i] = dot3((hi_ref[...], lo_ref[...]), split(cells))


def image_x_stage(place, grams, basis_s, product, cells):
    sa, gx, planes, own, eight, width = cells.shape
    columns = product.shape[2]
    half = jax.ShapeDtypeStruct((gx // 2, columns, width), F32)
    return pl.pallas_call(
        image_x_kernel,
        in_specs=[SMEM] + [VMEM] * 3 + [HBM],
        out_specs=[VMEM] * 3,
        out_shape=[jax.ShapeDtypeStruct(basis_s.shape, F32), half, half],
        scratch_shapes=[pltpu.VMEM((columns, planes * product.shape[1]), BF16)] * 2 + held(cells),
        compiler_params=PARAMS,
        name="factor_species_and_image_x",
    )(place, grams, basis_s, product, pltpu.with_memory_space_constraint(cells, pltpu.HBM))


def first_kernel(factor_ref, cells_ref, out_ref, hi_ref, lo_ref, held_ref, sems):
    copies = bring(cells_ref, held_ref, sems)
    species, rank = factor_ref.shape
    low = hi_ref.shape[0]
    hi_ref[...], lo_ref[...] = mixing(factor_ref[...], species, rank)
    for g in range(cells_ref.shape[1]):
        copies[g].wait()
        for p, cells in enumerate(planes_of(held_ref, g)):
            out_ref[g, p * low : (p + 1) * low, :] = dot3((hi_ref[...], lo_ref[...]), split(cells))


def first_stage(factor, cells):
    sa, gx, planes, own, eight, width = cells.shape
    species, rank = factor.shape
    low, wide = rank * 8, species * 8
    return pl.pallas_call(
        first_kernel,
        in_specs=[VMEM, HBM],
        out_specs=VMEM,
        out_shape=jax.ShapeDtypeStruct((gx, planes * low, width), F32),
        scratch_shapes=[pltpu.VMEM((low, wide), BF16)] * 2 + held(cells),
        compiler_params=PARAMS,
        cost_estimate=cost(3 * 2 * planes * low * wide * gx * width, 4 * (cells.size + gx * planes * low * width)),
        name="first",
    )(factor, pltpu.with_memory_space_constraint(cells, pltpu.HBM))


def second_kernel(place_ref, own_ref, other_ref, first_ref, factor_ref, send_ref, work_ref, hold_ref):
    half, rank, width = own_ref.shape
    gx, n = 2 * half, rank
    xl, y, c = place_ref[0], place_ref[1], place_ref[2]
    norms = jnp.zeros((n, n), F32)
    raw = jnp.zeros(hold_ref.shape, F32)
    for image_ref, start in ((own_ref, c * half), (other_ref, (1 - c) * half)):
        for i in range(half):
            norms += exact(image_ref[i], image_ref[i], NT)
            raw += dot3(split(first_ref[start + i]), split(image_ref[i]), NT)
    hold_ref[...] = raw
    fill(work_ref, norms)
    inverse = invert_factor(work_ref, n, 64)
    factor_ref[...] = exact(inverse, jnp.where(xl == c, own_ref[y], other_ref[y])).T
    second = exact(hold_ref[...], inverse, NT)
    hold_ref[...] = second
    groups = send_ref.shape[0] // gx
    each = 3
    lane = iota((8, 128), 1)
    for g in range(groups):
        for half in range(n // 128):
            tiles = [
                hold_ref[(g * each + j) * 8 : (g * each + j + 1) * 8, half * 128 : (half + 1) * 128]
                for j in range(each)
            ]
            for part in range(4):
                moved = [
                    tile if (j - part) % 4 == 0 else pltpu.roll(tile, ((j - part) % 4) * 32, 1)
                    for j, tile in enumerate(tiles)
                ]
                mixed = jnp.where(lane < 32, moved[0], jnp.where(lane < 64, moved[1], moved[2]))
                send_ref[g * gx + half * 4 + part] = jnp.where(lane < 96, mixed, 0.0)


def second_stage(place, own, other, first):
    half, rank, width = own.shape
    rows = first.shape[1]
    return pl.pallas_call(
        second_kernel,
        in_specs=[SMEM, VMEM, VMEM, VMEM],
        out_specs=[VMEM] * 2,
        out_shape=[
            jax.ShapeDtypeStruct((width, rank), F32),
            jax.ShapeDtypeStruct((rows // 24 * 2 * half, 8, 128), F32),
        ],
        scratch_shapes=[pltpu.VMEM((rank, 2 * rank), F32), pltpu.VMEM((rows, rank), F32)],
        compiler_params=PARAMS,
        name="factor_x_and_second",
    )(place, own, other, first)


def image_y_kernel(place_ref, near_ref, far_ref, near_o_ref, far_o_ref, second_ref, keep_ref, give_ref, basis_ref):
    xh, c, z = place_ref[3], place_ref[2], place_ref[4]
    count = near_ref.shape[0]
    for piece_ref, over, across in (
        (near_ref, xh, c), (far_ref, 1 - xh, c), (near_o_ref, xh, 1 - c), (far_o_ref, 1 - xh, 1 - c)
    ):
        for k in range(count):
            basis_ref[(over * 2 + across) * count + lax.rem(z + k, count)] = piece_ref[k]
    rows = second_ref.shape[0]
    turned = second_ref[...].T
    both = split(turned)
    inner = dot3(both, split(basis_ref[...].reshape(rows, basis_ref.shape[2])))
    left = split(inner.T)
    half, rank, width = keep_ref.shape
    for b in range(2 * half):
        cols = slice(b * width, (b + 1) * width)
        image = dot3(left, (both[0][:, cols], both[1][:, cols]))

        @pl.when(b // half == c)
        def _():
            keep_ref[b % half] = image

        @pl.when(b // half != c)
        def _():
            give_ref[b % half] = image


def image_y_stage(place, pieces, second):
    rank = pieces[0].shape[2]
    count, each = pieces[0].shape[:2]
    shape = jax.ShapeDtypeStruct((second.shape[0] // 512, rank, 256), F32)
    return pl.pallas_call(
        image_y_kernel,
        in_specs=[SMEM] + [VMEM] * 5,
        out_specs=[VMEM] * 2,
        out_shape=[shape, shape],
        scratch_shapes=[pltpu.VMEM((4 * count, each, rank), F32)],
        compiler_params=PARAMS,
        name="image_y",
    )(place, *pieces, second)


def core_kernel(place_ref, own_ref, other_ref, second_ref, factor_ref, core_ref, work_ref, turn_ref):
    half, n, width = own_ref.shape
    xh, c, z = place_ref[3], place_ref[2], place_ref[4]
    norms = jnp.zeros((n, n), F32)
    raw = jnp.zeros((n, second_ref.shape[1]), F32)
    for image_ref, start in ((own_ref, c * half), (other_ref, (1 - c) * half)):
        for b in range(half):
            image = image_ref[b]
            norms += exact(image, image, NT)
            first_row = pl.multiple_of((start + b) * width, width)
            raw += exact(image, second_ref[pl.ds(first_row, width), :])
    fill(work_ref, norms)
    inverse = invert_factor(work_ref, n, 64)
    core_ref[...] = exact(inverse, raw)
    turn_ref[...] = exact(inverse, jnp.where(xh == c, own_ref[c], other_ref[c])).T
    count = factor_ref.shape[0]
    factor_ref[...] = turn_ref[pl.ds(pl.multiple_of(z * count, count), count), :]


def core_stage(place, own, other, second, count):
    half, n, width = own.shape
    return pl.pallas_call(
        core_kernel,
        in_specs=[SMEM, VMEM, VMEM, VMEM],
        out_specs=[VMEM] * 2,
        out_shape=[
            jax.ShapeDtypeStruct((count, n), F32),
            jax.ShapeDtypeStruct((n, second.shape[1]), F32),
        ],
        scratch_shapes=[pltpu.VMEM((n, 2 * n), F32), pltpu.VMEM((width, n), F32)],
        compiler_params=PARAMS,
        name="factor_y_and_core",
    )(place, own, other, second)


def swap(parts, axes):
    return lax.all_to_all(parts, axes, split_axis=0, concat_axis=0, tiled=True)


def spread(one, axes, count):
    return swap(jnp.broadcast_to(one, (count,) + one.shape), axes)


def shifted(x, axis, count, by):
    return lax.ppermute(x, axis, [((i + by) % count, i) for i in range(count)])


def around(x, axis, count):
    return jnp.stack([x] + [shifted(x, axis, count, k) for k in range(1, count)])


def copies_kernel(parts_ref, out_ref):
    out_ref[...] = jnp.broadcast_to(jnp.sum(parts_ref[...], axis=0, keepdims=True), out_ref.shape)


def copies_of_sum(parts, count):
    return pl.pallas_call(
        copies_kernel,
        in_specs=[VMEM],
        out_specs=VMEM,
        out_shape=jax.ShapeDtypeStruct((count,) + parts.shape[1:], F32),
        compiler_params=PARAMS,
        name="copies_of_sum",
    )(parts)


def pair_kernel(one_ref, other_ref, out_ref):
    out_ref[...] = jnp.broadcast_to((one_ref[...] + other_ref[...])[None], out_ref.shape)


def copies_of_pair(one, other, count):
    return pl.pallas_call(
        pair_kernel,
        in_specs=[VMEM] * 2,
        out_specs=VMEM,
        out_shape=jax.ShapeDtypeStruct((count,) + one.shape, F32),
        compiler_params=PARAMS,
        name="copies_of_pair",
    )(one, other)


def after_kernel(x_ref, ready_ref, out_ref):
    del x_ref, ready_ref, out_ref


def after(x, ready):
    return pl.pallas_call(
        after_kernel,
        in_specs=[HBM, HBM],
        out_specs=HBM,
        out_shape=jax.ShapeDtypeStruct(x.shape, x.dtype),
        input_output_aliases={0: 0},
        compiler_params=PARAMS,
        name="after",
    )(x, ready)


def total(keep, give, beside=lambda mine: (mine, ())):
    mine = keep + shifted(give, "c", 2, 1)
    mine = copies_of_sum(swap(mine.reshape(64, mine.size // (64 * 256), 256), CHIPS), 64)
    mine, extra = beside(mine)
    own = swap(mine, CHIPS).reshape(keep.shape)
    return own, shifted(own, "c", 2, 1), extra


def local(field, basis_s, basis_x, basis_y):
    gx_n, sa_n = 8, 4
    place = jnp.stack([lax.axis_index(a) for a in ("xl", "y", "c", "xh", "z")])
    rows = basis_x.shape[0] // 2
    near_x = around(lax.dynamic_slice_in_dim(basis_x, lax.axis_index("c") * rows, rows, 0), "y", 4)
    packed, near_x = lax.optimization_barrier((pack(field, gx_n * sa_n), near_x))
    cells = swap(packed, ("z",) + GX)
    cells = cells.reshape((sa_n, gx_n) + cells.shape[1:])
    near_x, cells = lax.optimization_barrier((near_x, cells))
    far_x = shifted(near_x, "xl", 2, 1)
    partial = gram(cells)
    partial = copies_of_pair(partial, shifted(partial, "c", 2, 1), 64)
    far_x = after(far_x, partial)
    pieces_x = (near_x, far_x, shifted(near_x, "c", 2, 1), shifted(far_x, "c", 2, 1))
    grams = swap(partial, CHIPS)
    product = based(place, pieces_x, cells)
    factor_s, keep, give = image_x_stage(place, grams, basis_s, product, cells)
    give, late_y = lax.optimization_barrier((give, basis_y))
    first = first_stage(factor_s, cells)
    near_y = around(late_y, "z", 4)

    def beside(mine):
        mine, ready, near = lax.optimization_barrier((mine, first, near_y))
        return mine, (ready, near, shifted(near, "xh", 2, 1))

    own, other, (first, near_y, far_y) = total(keep, give, beside)
    factor_x, send = second_stage(place, own, other, first)
    second = swap(send, GY + ("z",) + GX).reshape(-1, 128)
    pieces_y = (near_y, far_y, shifted(near_y, "c", 2, 1), shifted(far_y, "c", 2, 1))
    own, other, _ = total(*image_y_stage(place, pieces_y, second))
    factor_y, core = core_stage(place, own, other, second, basis_y.shape[0])
    rank_y = core.shape[0]
    blocks = swap(core.reshape(16, rank_y // 16, 128), GY + ("z",))
    core = blocks.reshape(2, 8, rank_y // 16, 4, 32)[:, :, :, :3, :]
    core = core.transpose(2, 4, 1, 3, 0).reshape(rank_y // 16, 32, 24, 2)
    return core, factor_s, factor_x, factor_y


def solution(mesh):
    fine = Mesh(mesh.devices.reshape(2, 4, 2, 2, 4), ("xl", "y", "xh", "c", "z"))
    yz = GY + ("z",)
    return jax.shard_map(
        local,
        mesh=fine,
        in_specs=(P("z", None, GX, GY), P(), P(GX, None), P(yz, None)),
        out_specs=(P(yz, GX, None, None), P(), P(GX, None), P(yz, None)),
        check_vma=False,
    )
```
